512 devices in a mesh: gx: 4 (over y), gy: 16 (over z_lo, core), gz: 8 (over x, z_hi).
Axes of the slice: x: 4, y: 4, z: 16 (z_hi: 2, z_lo: 8; z = z_hi * 8 + z_lo), core: 2. Of those that a mesh axis runs over, the one named last changes fastest.
Arguments:
- mixture_fractions: float32 [4, 128, 768, 512], P(None, 'gy', 'gz', 'gx'), may hold values from 0 to 1
- velocity: float32 [3, 128, 768, 512], P(None, 'gy', 'gz', 'gx'), may hold values from -3 to 3
Outputs:
- updated: float32 [4, 128, 768, 512], P(None, 'gy', 'gz', 'gx')
- gram: float32 [512, 512], P('gx')
The draws below stay inside these ranges and needn't reach their ends.
All inputs are finite; a program needn't handle non-finite values.
Results may differ from the reference program's by a relative error of at most 0.00005.
Values sent between devices are 32-bit elements; how exact they have to be, the bound alone decides.
No kernel may reach another device: no remote copies, remote signals or barrier semaphores. Data moves between devices by JAX's collectives and lax.ppermute only.
A program may use at most 64 MiB of HBM per device.

```python
import math
from functools import partial
import jax
import jax.numpy as jnp
from jax import lax

SPECIES_COUNT = 4
CX = 128
CY = 8
CZ = 96
NX = 512
NY = 128
NZ = 768


def one_species(subkey, level, rough, common_seed, wave):
    key_noise, key_common, key_counts, key_phase = jax.random.split(subkey, 4)
    noise = jax.random.uniform(key_noise, (NY, NZ, NX), jnp.float32, -rough, rough)
    joint_key = jax.random.uniform(key_common, (NY, NZ, NX), jnp.float32, -common_seed, common_seed)
    lag_one = CX + CX // 4 + 1
    lag_two = 2 * CX + CX // 2 + 3
    field = level + noise + joint_key + jnp.roll(joint_key, lag_one, 2) + jnp.roll(joint_key, lag_two, 2)
    counts = jax.random.randint(key_counts, (2, 3), 1, 3).astype(jnp.float32)
    phase_angles = jax.random.uniform(key_phase, (2,), jnp.float32, 0.0, 2.0 * math.pi)
    xs = jnp.arange(NX, dtype=jnp.float32) / NX
    ys = jnp.arange(NY, dtype=jnp.float32) / NY
    zs = jnp.arange(NZ, dtype=jnp.float32) / NZ
    for species_number in range(2):
        angle = counts[species_number, 0] * xs[None, None, :] + counts[species_number, 1] * (NY // CY) * ys[:, None, None]
        angle = angle + counts[species_number, 2] * (NZ // CZ) * zs[None, :, None]
        field = field + wave * jnp.cos(2.0 * math.pi * angle + phase_angles[species_number])
    return field


def draw_mixture_fractions(key, part):
    key = jax.random.fold_in(key, 11)
    level, rough, common_seed, wave = (0.5, 0.05, 0.12, 0.04)
    subkeys = jax.random.split(key, SPECIES_COUNT)
    maker = partial(one_species, level=level, rough=rough, common_seed=common_seed, wave=wave)
    return lax.map(maker, subkeys).astype(jnp.float32)


def levels(key, shape, cuts, low, top_value):
    def one(position, parts):
        draws = jax.random.uniform(jax.random.fold_in(jax.random.fold_in(key, 6), position), (parts,), jnp.float32, low / len(cuts), top_value / len(cuts))
        return jnp.repeat(jnp.exp(draws), shape[position] // parts).reshape((-1,) + (1,) * (len(shape) - position - 1))

    gain = one(*cuts[0])
    for cut in cuts[1:]:
        gain = gain * one(*cut)
    return gain


def normal_values(stream_key, extent, deviation, bound, cuts=(), kind=jnp.bfloat16):
    values = deviation * jax.random.normal(stream_key, extent, jnp.float32)
    if cuts:
        values = values * levels(stream_key, extent, cuts, -0.22, 0.18)
    return jnp.clip(values, -bound, bound).astype(kind)


def setup_inputs(seed: int = 0) -> dict:
    key_list = jax.random.split(jax.random.key(seed), 3)
    return {
        "mixture_fractions": draw_mixture_fractions(jax.random.fold_in(key_list[2], 71), 0),
        "velocity": normal_values(key_list[1], (3, NY, NZ, NX), 0.5, 3.0, ((1, 16), (2, 8), (3, 4)), jnp.float32),
    }


leading_weight = (4.0 / 5.0, -1.0 / 5.0, 4.0 / 105.0, -1.0 / 280.0)
second_coef = (-205.0 / 72.0, 8.0 / 5.0, -1.0 / 5.0, 8.0 / 315.0, -1.0 / 560.0)


def derivs(field, axis):
    first = jnp.zeros_like(field)
    second_factor = second_coef[0] * field
    for step in range(1, 5):
        ahead = jnp.roll(field, -step, axis)
        behind = jnp.roll(field, step, axis)
        first = first + leading_weight[step - 1] * (ahead - behind)
        second_factor = second_factor + second_coef[step] * (ahead + behind)
    return first, second_factor


def reference(mixture_fractions, velocity):
    diffusion = jnp.array([0.10, 0.12, 0.08, 0.15], jnp.float32)
    stoichiometry = jnp.array([-1.0, -1.0, 2.0, 0.0], jnp.float32)

    def transport(packed):
        field, coef = packed
        dx1, dx2 = derivs(field, 2)
        dy1, dy2 = derivs(field, 0)
        dz1, dz2 = derivs(field, 1)
        moved = velocity[0] * dx1 + velocity[1] * dy1 + velocity[2] * dz1
        return -moved + coef * (dx2 + dy2 + dz2)

    carried = lax.map(transport, (mixture_fractions, diffusion))
    heat_profile = 1.0 + 3.0 * mixture_fractions[2]
    burning_speed = 4.0 * mixture_fractions[0] * mixture_fractions[1] * jnp.exp(-3.0 / heat_profile)
    updated = mixture_fractions + 0.25 * (carried + stoichiometry[:, None, None, None] * burning_speed[None])
    unfold = updated.reshape(SPECIES_COUNT * NY * NZ, NX)
    total = lax.dot_general(unfold, unfold, (((0,), (0,)), ((), ())), precision=lax.Precision.HIGHEST, preferred_element_type=jnp.float32)
    gram = total * (1.0 / (SPECIES_COUNT * NY * NZ))
    return updated, gram
```

```python
import numpy as np
import jax
import jax.numpy as jnp
from jax import lax
from jax.experimental import pallas as pl
from jax.experimental.pallas import tpu as pltpu
from jax.sharding import Mesh, PartitionSpec as P

C1 = (4.0 / 5.0, -1.0 / 5.0, 4.0 / 105.0, -1.0 / 280.0)
C2 = (-205.0 / 72.0, 8.0 / 5.0, -1.0 / 5.0, 8.0 / 315.0, -1.0 / 560.0)
DIFF = (0.10, 0.12, 0.08, 0.15)
NU = (-1.0, -1.0, 2.0, 0.0)
PAIRS = [(a, b) for a in range(4) for b in range(a, 4)]
MIB = 1 << 20


def split(value):
    high = value.astype(jnp.bfloat16)
    return high, (value - high.astype(jnp.float32)).astype(jnp.bfloat16)


def x_matrix(width):
    matrix = np.zeros((2 * width, 2 * width))
    for i in range(width):
        for k in range(-4, 5):
            j = i + k
            row = j if 0 <= j < width else (width + 4 + j if j < 0 else width + 4 + j - width)
            if k:
                matrix[row, i] += np.sign(k) * C1[abs(k) - 1]
            matrix[row, width + i] += C2[abs(k)]
    return jnp.asarray(matrix, jnp.float32)


def dot(left, right):
    return lax.dot_general(
        left, right, (((1,), (0,)), ((), ())), preferred_element_type=jnp.float32
    )


def stencil_body(y, vel, ylow, yhigh, zlow, zhigh, xlow, xhigh, mh, ml, out, rate, side, dx, pad):
    count, rows, depth, width = y.shape
    side[...] = jnp.zeros_like(side)
    for j in range(rows):
        heat = 1.0 + 3.0 * y[2, j]
        rate[j] = y[0, j] * y[1, j] * jnp.exp(-3.0 / heat)

    def species(s, carry):
        diff = jnp.float32(0.25 * DIFF[0])
        nu = jnp.float32(NU[0])
        for q in range(1, count):
            diff = jnp.where(s == q, jnp.float32(0.25 * DIFF[q]), diff)
            nu = jnp.where(s == q, jnp.float32(NU[q]), nu)
        for j in range(rows):
            both = jnp.concatenate([xlow[s, j], xhigh[s, j]], axis=0)
            side[j * depth : (j + 1) * depth, 0:8] = both.T[:depth]
        left = jnp.concatenate([y[s].reshape(rows * depth, width), side[...]], axis=1)
        high, low = split(left)
        dx[...] = dot(high, mh[...]) + (dot(low, mh[...]) + dot(high, ml[...]))
        for j in range(rows):

            def layer(t):
                if t < 0:
                    return ylow[s, 4 + t]
                return y[s, t] if t < rows else yhigh[s, t - rows]

            slot = j % 2
            centre = y[s, j]
            pad[slot, 4:8] = zlow[s, j]
            pad[slot, 8 : 8 + depth] = centre
            pad[slot, 8 + depth : 12 + depth] = zhigh[s, j]
            d1y = d1z = None
            second = (2.0 * C2[0]) * centre + dx[j * depth : (j + 1) * depth, width:]
            for k in range(1, 5):
                ya, yb = layer(j + k), layer(j - k)
                za = pad[slot, 8 + k : 8 + k + depth]
                zb = pad[slot, 8 - k : 8 - k + depth]
                ty, tz = C1[k - 1] * (ya - yb), C1[k - 1] * (za - zb)
                d1y = ty if d1y is None else d1y + ty
                d1z = tz if d1z is None else d1z + tz
                second = second + C2[k] * ((ya + yb) + (za + zb))
            moved = vel[0, j] * dx[j * depth : (j + 1) * depth, :width]
            moved = moved + vel[1, j] * d1y + vel[2, j] * d1z
            out[s, j] = centre + (diff * second - 0.25 * moved + nu * rate[j])
        return carry

    lax.fori_loop(0, count, species, 0)


def stencil(y, vel, *rest):
    _, rows, depth, width = y.shape
    return pl.pallas_call(
        stencil_body,
        out_shape=jax.ShapeDtypeStruct(y.shape, jnp.float32),
        in_specs=[pl.BlockSpec(memory_space=pltpu.VMEM)] * 10,
        out_specs=pl.BlockSpec(memory_space=pltpu.VMEM),
        scratch_shapes=[
            pltpu.VMEM((rows, depth, width), jnp.float32),
            pltpu.VMEM((rows * depth, width), jnp.float32),
            pltpu.VMEM((rows * depth, 2 * width), jnp.float32),
            pltpu.VMEM((2, depth + 16, width), jnp.float32),
        ],
        compiler_params=pltpu.CompilerParams(vmem_limit_bytes=40 * MIB),
        name="stencil",
    )(y, vel, *rest)


def gram_body(lines, out):
    parts = lines.shape[0]
    whole = jnp.concatenate([lines[a] for a in range(parts)], axis=1)
    high, low = split(whole)
    turned_high, turned_low = split(whole.T)
    total = dot(turned_high, high) + (dot(turned_high, low) + dot(turned_low, high))
    for p, (a, b) in enumerate(PAIRS):
        out[p * 128 : (p + 1) * 128] = total[a * 128 : (a + 1) * 128, b * 128 : (b + 1) * 128]


def gram_blocks(lines):
    return pl.pallas_call(
        gram_body,
        out_shape=jax.ShapeDtypeStruct((len(PAIRS) * 128, 128), jnp.float32),
        in_specs=[pl.BlockSpec(memory_space=pltpu.VMEM)],
        out_specs=pl.BlockSpec(memory_space=pltpu.VMEM),
        compiler_params=pltpu.CompilerParams(vmem_limit_bytes=40 * MIB),
        name="gram",
    )(lines)


def rows_body(scale, place, blocks, out):
    mine = place[0]
    for b in range(4):
        low, top = jnp.minimum(mine, b), jnp.maximum(mine, b)
        index = low * 4 - (low * (low - 1)) // 2 + (top - low)
        tile = blocks[pl.ds(pl.multiple_of(index * 128, 128), 128)] * scale
        out[:, b * 128 : (b + 1) * 128] = jnp.where(mine <= b, tile, tile.T)


def gram_rows(blocks, place, scale):
    import functools

    return pl.pallas_call(
        functools.partial(rows_body, scale),
        out_shape=jax.ShapeDtypeStruct((128, 512), jnp.float32),
        in_specs=[
            pl.BlockSpec(memory_space=pltpu.SMEM),
            pl.BlockSpec(memory_space=pltpu.VMEM),
        ],
        out_specs=pl.BlockSpec(memory_space=pltpu.VMEM),
        name="gram_rows",
    )(place, blocks)


def exchange(pieces, axes):
    return lax.all_to_all(pieces, axes, split_axis=0, concat_axis=0, tiled=True)


def shards(y, vel):
    species, rows, depth, width = y.shape
    gy, gz, gx = ("zlo", "core"), ("x", "zhi"), ("gx",)

    def moves(axes, count):
        up = [(i, (i + 1) % count) for i in range(count)]
        return up, [(target, source) for source, target in up]

    up, down = moves(gz, 8)
    zlow = lax.ppermute(y[:, :, depth - 4 :], gz, up)
    zhigh = lax.ppermute(y[:, :, :4], gz, down)
    up, down = moves(gy, 16)
    ylow = lax.ppermute(y[:, rows - 4 :], gy, up)
    yhigh = lax.ppermute(y[:, :4], gy, down)
    up, down = moves(gx, 4)

    def face(part):
        turned = jnp.transpose(part, (0, 1, 3, 2))
        return jnp.pad(turned, ((0, 0), (0, 0), (0, 0), (0, 128 - depth)))

    xlow = lax.ppermute(face(y[..., width - 4 :]), gx, up)
    xhigh = lax.ppermute(face(y[..., :4]), gx, down)
    mh, ml = split(x_matrix(width))
    updated = stencil(y, vel, ylow, yhigh, zlow, zhigh, xlow, xhigh, mh, ml)

    lines = exchange(updated.reshape(4, species * rows * depth // 4, width), gx)
    blocks = gram_blocks(lines)
    plane, column = ("gx", "core", "x"), ("zlo", "zhi")
    part = jnp.sum(exchange(blocks.reshape(32, -1, 128), plane), axis=0)
    part = jnp.sum(exchange(jnp.broadcast_to(part, (16,) + part.shape), column), axis=0)
    blocks = exchange(jnp.broadcast_to(part, (32,) + part.shape), plane)
    place = lax.axis_index("gx").astype(jnp.int32).reshape(1)
    cells = species * rows * 16 * depth * 8
    return updated, gram_rows(blocks.reshape(-1, 128), place, 1.0 / cells)


def solution(mesh):
    fine = Mesh(mesh.devices.reshape(4, 8, 2, 4, 2), ("gx", "zlo", "core", "x", "zhi"))
    grid = P(None, ("zlo", "core"), ("x", "zhi"), "gx")
    return jax.shard_map(
        shards, mesh=fine, in_specs=(grid, grid), out_specs=(grid, P("gx", None)), check_vma=False
    )
```

```python
import functools

import ml_dtypes
import numpy as np
import jax
import jax.numpy as jnp
from jax import lax
from jax.experimental import pallas as pl
from jax.experimental.pallas import tpu as pltpu
from jax.sharding import Mesh, PartitionSpec as P

C1 = (4.0 / 5.0, -1.0 / 5.0, 4.0 / 105.0, -1.0 / 280.0)
C2 = (-205.0 / 72.0, 8.0 / 5.0, -1.0 / 5.0, 8.0 / 315.0, -1.0 / 560.0)
DIFF = (0.10, 0.12, 0.08, 0.15)
NU = (-1.0, -1.0, 2.0, 0.0)
PAIRS = [(a, b) for a in range(4) for b in range(a, 4)]
MIB = 1 << 20


def split(value):
    high = value.astype(jnp.bfloat16)
    return high, (value - high.astype(jnp.float32)).astype(jnp.bfloat16)


def x_matrices(width):
    matrix = np.zeros((2 * width, 2 * width))
    for i in range(width):
        for k in range(-4, 5):
            j = i + k
            row = j if 0 <= j < width else (width + 4 + j if j < 0 else width + 4 + j - width)
            if k:
                matrix[row, i] += np.sign(k) * C1[abs(k) - 1]
            matrix[row, width + i] += C2[abs(k)]
    matrix = matrix.astype(np.float32)
    high = matrix.astype(ml_dtypes.bfloat16)
    return high, (matrix - high.astype(np.float32)).astype(ml_dtypes.bfloat16)


def dot(left, right):
    return lax.dot_general(
        left, right, (((1,), (0,)), ((), ())), preferred_element_type=jnp.float32
    )


def lanes():
    return lax.broadcasted_iota(jnp.int32, (8, 128), 1)


def pack_body(place, y, inner, outer, za, zb, xs):
    count, rows, depth, width = y.shape
    core, half = place[1], place[2]
    lane = lanes()

    def species(s, carry):
        inner[s] = y[s, pl.ds(4 * (1 - core), 4)]
        outer[s] = y[s, pl.ds(4 * core, 4)]
        for j in range(rows):
            low, high = y[s, j, 0:4], y[s, j, depth - 4 :]
            at = 4 * (j % 2)
            za[s, j // 2, at : at + 4] = jnp.where(half == 0, high, low)
            zb[s, j // 2, at : at + 4] = jnp.where(half == 0, low, high)
            packed = jnp.zeros((8, width), jnp.float32)
            for g in range(depth // 8):
                turned = pltpu.roll(y[s, j, 8 * g : 8 * g + 8], 8 * g + 4, 1)
                packed = jnp.where(lane // 8 == g, turned, packed)
            xs[s, j] = packed
        return carry

    lax.fori_loop(0, count, species, 0)


SMEM = pl.BlockSpec(memory_space=pltpu.SMEM)
VMEM = pl.BlockSpec(memory_space=pltpu.VMEM)


def pack(place, y):
    count, rows, depth, width = y.shape
    shapes = [(count, 4, depth, width)] * 2 + [(count, rows // 2, 8, width)] * 2
    shapes = shapes + [(count, rows, 8, width)]
    return pl.pallas_call(
        pack_body,
        out_shape=[jax.ShapeDtypeStruct(shape, jnp.float32) for shape in shapes],
        in_specs=[SMEM, VMEM],
        out_specs=[VMEM] * 5,
        compiler_params=pltpu.CompilerParams(vmem_limit_bytes=24 * MIB),
        name="pack",
    )(place, y)


def stencil_body(place, y, vel, inner, outer, za, zb, xlow, xhigh, mh, ml, out, rate, side, dx, pad):
    count, rows, depth, width = y.shape
    core, half = place[1], place[2]
    below = lanes() % 8 < 4
    for j in range(rows):
        heat = 1.0 + 3.0 * y[2, j]
        rate[j] = y[0, j] * y[1, j] * jnp.exp(-3.0 / heat)

    def species(s, carry):
        diff = jnp.float32(0.25 * DIFF[0])
        nu = jnp.float32(NU[0])
        for q in range(1, count):
            diff = jnp.where(s == q, jnp.float32(0.25 * DIFF[q]), diff)
            nu = jnp.where(s == q, jnp.float32(NU[q]), nu)
        pad[pl.ds(12 * (1 - core), 4), 8 : 8 + depth] = inner[s]
        pad[pl.ds(12 * core, 4), 8 : 8 + depth] = outer[s]
        for j in range(rows):
            at = 4 * (j % 2)
            fa, fb = za[s, j // 2, at : at + 4], zb[s, j // 2, at : at + 4]
            pad[4 + j, 4:8] = jnp.where(half == 0, fb, fa)
            pad[4 + j, 8 : 8 + depth] = y[s, j]
            pad[4 + j, 8 + depth : 12 + depth] = jnp.where(half == 0, fa, fb)
            packed = jnp.where(below, xlow[s, j], xhigh[s, j])
            for g in range(depth // 8):
                row = j * depth + 8 * g
                side[row : row + 8] = pltpu.roll(packed, (128 - 8 * g) % 128, 1)
        left = jnp.concatenate([y[s].reshape(rows * depth, width), side[...]], axis=1)
        high, low = split(left)
        dx[...] = dot(high, mh[...]) + (dot(low, mh[...]) + dot(high, ml[...]))
        for j in range(rows):
            centre = y[s, j]
            d1y = d1z = None
            second = (2.0 * C2[0]) * centre + dx[j * depth : (j + 1) * depth, width:]
            for k in range(1, 5):
                ya, yb = pad[4 + j + k, 8 : 8 + depth], pad[4 + j - k, 8 : 8 + depth]
                za_, zb_ = pad[4 + j, 8 + k : 8 + k + depth], pad[4 + j, 8 - k : 8 - k + depth]
                ty, tz = C1[k - 1] * (ya - yb), C1[k - 1] * (za_ - zb_)
                d1y = ty if d1y is None else d1y + ty
                d1z = tz if d1z is None else d1z + tz
                second = second + C2[k] * ((ya + yb) + (za_ + zb_))
            moved = vel[0, j] * dx[j * depth : (j + 1) * depth, :width]
            moved = moved + vel[1, j] * d1y + vel[2, j] * d1z
            out[s, j] = centre + (diff * second - 0.25 * moved + nu * rate[j])
        return carry

    lax.fori_loop(0, count, species, 0)


def stencil(place, y, *rest):
    _, rows, depth, width = y.shape
    return pl.pallas_call(
        stencil_body,
        out_shape=jax.ShapeDtypeStruct(y.shape, jnp.float32),
        in_specs=[SMEM] + [VMEM] * (1 + len(rest)),
        out_specs=VMEM,
        scratch_shapes=[
            pltpu.VMEM((rows, depth, width), jnp.float32),
            pltpu.VMEM((rows * depth, width), jnp.float32),
            pltpu.VMEM((rows * depth, 2 * width), jnp.float32),
            pltpu.VMEM((rows + 8, depth + 16, width), jnp.float32),
        ],
        compiler_params=pltpu.CompilerParams(vmem_limit_bytes=40 * MIB),
        name="stencil",
    )(place, y, *rest)


def gram_body(place, lines, mine, other):
    parts = lines.shape[0]
    whole = jnp.concatenate([lines[a] for a in range(parts)], axis=1)
    high, low = split(whole)
    turned_high, turned_low = split(whole.T)
    total = dot(turned_high, high) + (dot(turned_high, low) + dot(turned_low, high))
    tiles = [total[a * 128 : (a + 1) * 128, b * 128 : (b + 1) * 128] for a, b in PAIRS]
    for q in range(5):
        first, second = tiles[q], tiles[q + 5]
        mine[q * 128 : (q + 1) * 128] = jnp.where(place[1] == 0, first, second)
        other[q * 128 : (q + 1) * 128] = jnp.where(place[1] == 0, second, first)


def gram_blocks(place, lines):
    return pl.pallas_call(
        gram_body,
        out_shape=[jax.ShapeDtypeStruct((len(PAIRS) * 64, 128), jnp.float32)] * 2,
        in_specs=[SMEM, VMEM],
        out_specs=[VMEM] * 2,
        compiler_params=pltpu.CompilerParams(vmem_limit_bytes=40 * MIB),
        name="gram",
    )(place, lines)


def rows_body(scale, place, mine, other, out):
    row, core = place[0], place[1]
    for b in range(4):
        low, top = jnp.minimum(row, b), jnp.maximum(row, b)
        index = low * 4 - (low * (low - 1)) // 2 + (top - low)
        owner = jnp.where(index >= 5, 1, 0)
        at = pl.ds(pl.multiple_of((index - 5 * owner) * 128, 128), 128)
        tile = jnp.where(owner == core, mine[at], other[at]) * scale
        out[:, b * 128 : (b + 1) * 128] = jnp.where(row <= b, tile, tile.T)


def gram_rows(place, mine, other, scale):
    return pl.pallas_call(
        functools.partial(rows_body, scale),
        out_shape=jax.ShapeDtypeStruct((128, 512), jnp.float32),
        in_specs=[SMEM, VMEM, VMEM],
        out_specs=VMEM,
        name="gram_rows",
    )(place, mine, other)


def exchange(pieces, axes):
    return lax.all_to_all(pieces, axes, split_axis=0, concat_axis=0, tiled=True)


def gather_sum(part, axes, count):
    return jnp.sum(exchange(jnp.broadcast_to(part, (count,) + part.shape), axes), axis=0)


def shards(y, vel):
    species, rows, depth, width = y.shape
    gy, gz, gx = ("zpair", "znear", "core"), ("x", "zhi"), ("gx",)
    place = jnp.stack([lax.axis_index("gx"), lax.axis_index("core"), lax.axis_index("zhi")])
    place = place.astype(jnp.int32)
    inner, outer, za, zb, xs = pack(place, y)

    def cross(count):
        return [(i, (i + 1) % count if i % 2 else (i - 1) % count) for i in range(count)]

    up = [(i, (i + 1) % 4) for i in range(4)]
    swap = [(0, 1), (1, 0)]
    za = lax.ppermute(za, "zhi", swap)
    zb = lax.ppermute(zb, gz, cross(8))
    outer = lax.ppermute(outer, gy, cross(16))
    inner = lax.ppermute(inner, "core", swap)
    xlow = lax.ppermute(xs, gx, up)
    xhigh = lax.ppermute(xs, gx, [(target, source) for source, target in up])
    updated = stencil(place, y, vel, inner, outer, za, zb, xlow, xhigh, *x_matrices(width))

    lines = exchange(updated.reshape(4, species * rows * depth // 4, width), gx)
    mine, other = gram_blocks(place, lines)
    mine = mine + lax.ppermute(other, "core", swap)
    plane = ("gx", "x")
    part = jnp.sum(exchange(mine.reshape(16, -1, 128), plane), axis=0)
    part = gather_sum(part, ("znear",), 4)
    part = gather_sum(part, ("zpair", "zhi"), 4)
    mine = exchange(jnp.broadcast_to(part, (16,) + part.shape), plane).reshape(-1, 128)
    other = lax.ppermute(mine, "core", swap)
    cells = species * rows * 16 * depth * 8
    return updated, gram_rows(place, mine, other, 1.0 / cells)


def solution(mesh):
    axes = ("gx", "zpair", "znear", "core", "x", "zhi")
    fine = Mesh(mesh.devices.reshape(4, 2, 4, 2, 4, 2), axes)
    grid = P(None, ("zpair", "znear", "core"), ("x", "zhi"), "gx")
    return jax.shard_map(
        shards, mesh=fine, in_specs=(grid, grid), out_specs=(grid, P("gx", None)), check_vma=False
    )
```

```python
import functools

import ml_dtypes
import numpy as np
import jax
import jax.numpy as jnp
from jax import lax
from jax.experimental import pallas as pl
from jax.experimental.pallas import tpu as pltpu
from jax.sharding import Mesh, PartitionSpec as P

C1 = (4.0 / 5.0, -1.0 / 5.0, 4.0 / 105.0, -1.0 / 280.0)
C2 = (-205.0 / 72.0, 8.0 / 5.0, -1.0 / 5.0, 8.0 / 315.0, -1.0 / 560.0)
DIFF = (0.10, 0.12, 0.08, 0.15)
NU = (-1.0, -1.0, 2.0, 0.0)
PAIRS = [(a, b) for a in range(4) for b in range(a, 4)]
MIB = 1 << 20


def split(value):
    high = value.astype(jnp.bfloat16)
    return high, (value - high.astype(jnp.float32)).astype(jnp.bfloat16)


def x_matrices(width):
    matrix = np.zeros((2 * width, 2 * width))
    for i in range(width):
        for k in range(-4, 5):
            j = i + k
            row = j if 0 <= j < width else (width + 4 + j if j < 0 else width + 4 + j - width)
            if k:
                matrix[row, i] += np.sign(k) * C1[abs(k) - 1]
            matrix[row, width + i] += C2[abs(k)]
    matrix = matrix.astype(np.float32)
    high = matrix.astype(ml_dtypes.bfloat16)
    return high, (matrix - high.astype(np.float32)).astype(ml_dtypes.bfloat16)


def dot(left, right):
    return lax.dot_general(
        left, right, (((1,), (0,)), ((), ())), preferred_element_type=jnp.float32
    )


def lanes():
    return lax.broadcasted_iota(jnp.int32, (8, 128), 1)


def pack_body(place, y, inner, outer, za, zb, xs):
    count, rows, depth, width = y.shape
    core, half = place[1], place[2]
    lane = lanes()

    def species(s, carry):
        inner[s] = y[s, pl.ds(4 * (1 - core), 4)]
        outer[s] = y[s, pl.ds(4 * core, 4)]
        for j in range(rows):
            low, high = y[s, j, 0:4], y[s, j, depth - 4 :]
            at = 4 * (j % 2)
            za[s, j // 2, at : at + 4] = jnp.where(half == 0, high, low)
            zb[s, j // 2, at : at + 4] = jnp.where(half == 0, low, high)
            packed = jnp.zeros((8, width), jnp.float32)
            for g in range(depth // 8):
                turned = pltpu.roll(y[s, j, 8 * g : 8 * g + 8], 8 * g + 4, 1)
                packed = jnp.where(lane // 8 == g, turned, packed)
            xs[s, j] = packed
        return carry

    lax.fori_loop(0, count, species, 0)


SMEM = pl.BlockSpec(memory_space=pltpu.SMEM)
VMEM = pl.BlockSpec(memory_space=pltpu.VMEM)


def pack(place, y):
    count, rows, depth, width = y.shape
    shapes = [(count, 4, depth, width)] * 2 + [(count, rows // 2, 8, width)] * 2
    shapes = shapes + [(count, rows, 8, width)]
    return pl.pallas_call(
        pack_body,
        out_shape=[jax.ShapeDtypeStruct(shape, jnp.float32) for shape in shapes],
        in_specs=[SMEM, VMEM],
        out_specs=[VMEM] * 5,
        compiler_params=pltpu.CompilerParams(vmem_limit_bytes=24 * MIB),
        name="pack",
    )(place, y)


def factors(s, count):
    diff = jnp.float32(0.25 * DIFF[0])
    nu = jnp.float32(NU[0])
    for q in range(1, count):
        diff = jnp.where(s == q, jnp.float32(0.25 * DIFF[q]), diff)
        nu = jnp.where(s == q, jnp.float32(NU[q]), nu)
    return diff, nu


def along_z_body(place, y, vel, za, zb, out, rate, pad):
    count, rows, depth, width = y.shape
    half = place[2]
    for j in range(rows):
        heat = 1.0 + 3.0 * y[2, j]
        rate[j] = y[0, j] * y[1, j] * jnp.exp(-3.0 / heat)

    def species(s, carry):
        diff, nu = factors(s, count)
        for j in range(rows):
            at = 4 * (j % 2)
            fa, fb = za[s, j // 2, at : at + 4], zb[s, j // 2, at : at + 4]
            pad[j, 4:8] = jnp.where(half == 0, fb, fa)
            pad[j, 8 : 8 + depth] = y[s, j]
            pad[j, 8 + depth : 12 + depth] = jnp.where(half == 0, fa, fb)
        for j in range(rows):
            centre = y[s, j]
            first = None
            second = (2.0 * C2[0]) * centre
            for k in range(1, 5):
                ahead, behind = pad[j, 8 + k : 8 + k + depth], pad[j, 8 - k : 8 - k + depth]
                term = (0.25 * C1[k - 1]) * (ahead - behind)
                first = term if first is None else first + term
                second = second + C2[k] * (ahead + behind)
            out[s, j] = centre + (diff * second - vel[2, j] * first + nu * rate[j])
        return carry

    lax.fori_loop(0, count, species, 0)


def along_z(place, y, *rest):
    _, rows, depth, width = y.shape
    return pl.pallas_call(
        along_z_body,
        out_shape=jax.ShapeDtypeStruct(y.shape, jnp.float32),
        in_specs=[SMEM] + [VMEM] * (1 + len(rest)),
        out_specs=VMEM,
        scratch_shapes=[
            pltpu.VMEM((rows, depth, width), jnp.float32),
            pltpu.VMEM((rows, depth + 16, width), jnp.float32),
        ],
        compiler_params=pltpu.CompilerParams(vmem_limit_bytes=24 * MIB),
        cost_estimate=pl.CostEstimate(
            flops=10**10, bytes_accessed=2 * 10**8, transcendentals=0
        ),
        name="along_z",
    )(place, y, *rest)


def along_xy_body(place, y, vel, base, outer, inner, xlow, xhigh, mh, ml, out, side, dx, pad):
    count, rows, depth, width = y.shape
    core = place[1]
    below = lanes() % 8 < 4

    def species(s, carry):
        diff, _ = factors(s, count)
        pad[pl.ds(12 * (1 - core), 4)] = inner[s]
        pad[pl.ds(12 * core, 4)] = outer[s]
        pad[4 : 4 + rows] = y[s]
        for j in range(rows):
            packed = jnp.where(below, xlow[s, j], xhigh[s, j])
            for g in range(depth // 8):
                row = j * depth + 8 * g
                side[row : row + 8] = pltpu.roll(packed, (128 - 8 * g) % 128, 1)
        left = jnp.concatenate([y[s].reshape(rows * depth, width), side[...]], axis=1)
        high, low = split(left)
        dx[...] = dot(high, mh[...]) + (dot(low, mh[...]) + dot(high, ml[...]))
        for j in range(rows):
            first = None
            second = dx[j * depth : (j + 1) * depth, width:]
            for k in range(1, 5):
                ahead, behind = pad[4 + j + k], pad[4 + j - k]
                term = (0.25 * C1[k - 1]) * (ahead - behind)
                first = term if first is None else first + term
                second = second + C2[k] * (ahead + behind)
            moved = (0.25 * vel[0, j]) * dx[j * depth : (j + 1) * depth, :width]
            out[s, j] = base[s, j] + (diff * second - (moved + vel[1, j] * first))
        return carry

    lax.fori_loop(0, count, species, 0)


def along_xy(place, y, *rest):
    _, rows, depth, width = y.shape
    return pl.pallas_call(
        along_xy_body,
        out_shape=jax.ShapeDtypeStruct(y.shape, jnp.float32),
        in_specs=[SMEM] + [VMEM] * (1 + len(rest)),
        out_specs=VMEM,
        scratch_shapes=[
            pltpu.VMEM((rows * depth, width), jnp.float32),
            pltpu.VMEM((rows * depth, 2 * width), jnp.float32),
            pltpu.VMEM((rows + 8, depth, width), jnp.float32),
        ],
        compiler_params=pltpu.CompilerParams(vmem_limit_bytes=32 * MIB),
        name="along_xy",
    )(place, y, *rest)


def gram_body(place, lines, mine, other):
    parts = lines.shape[0]
    whole = jnp.concatenate([lines[a] for a in range(parts)], axis=1)
    high, low = split(whole)
    turned_high, turned_low = split(whole.T)
    total = dot(turned_high, high) + (dot(turned_high, low) + dot(turned_low, high))
    tiles = [total[a * 128 : (a + 1) * 128, b * 128 : (b + 1) * 128] for a, b in PAIRS]
    for q in range(5):
        first, second = tiles[q], tiles[q + 5]
        mine[q * 128 : (q + 1) * 128] = jnp.where(place[1] == 0, first, second)
        other[q * 128 : (q + 1) * 128] = jnp.where(place[1] == 0, second, first)


def gram_blocks(place, lines):
    return pl.pallas_call(
        gram_body,
        out_shape=[jax.ShapeDtypeStruct((len(PAIRS) * 64, 128), jnp.float32)] * 2,
        in_specs=[SMEM, VMEM],
        out_specs=[VMEM] * 2,
        compiler_params=pltpu.CompilerParams(vmem_limit_bytes=40 * MIB),
        name="gram",
    )(place, lines)


def rows_body(scale, place, mine, other, out):
    row, core = place[0], place[1]
    for b in range(4):
        low, top = jnp.minimum(row, b), jnp.maximum(row, b)
        index = low * 4 - (low * (low - 1)) // 2 + (top - low)
        owner = jnp.where(index >= 5, 1, 0)
        at = pl.ds(pl.multiple_of((index - 5 * owner) * 128, 128), 128)
        tile = jnp.where(owner == core, mine[at], other[at]) * scale
        out[:, b * 128 : (b + 1) * 128] = jnp.where(row <= b, tile, tile.T)


def gram_rows(place, mine, other, scale):
    return pl.pallas_call(
        functools.partial(rows_body, scale),
        out_shape=jax.ShapeDtypeStruct((128, 512), jnp.float32),
        in_specs=[SMEM, VMEM, VMEM],
        out_specs=VMEM,
        name="gram_rows",
    )(place, mine, other)


def exchange(pieces, axes):
    return lax.all_to_all(pieces, axes, split_axis=0, concat_axis=0, tiled=True)


def gather_sum(part, axes, count):
    return jnp.sum(exchange(jnp.broadcast_to(part, (count,) + part.shape), axes), axis=0)


def shards(y, vel):
    species, rows, depth, width = y.shape
    gy, gz, gx = ("zpair", "znear", "core"), ("x", "zhi"), ("gx",)
    place = jnp.stack([lax.axis_index("gx"), lax.axis_index("core"), lax.axis_index("zhi")])
    place = place.astype(jnp.int32)
    inner, outer, za, zb, xs = pack(place, y)

    def cross(count):
        return [(i, (i + 1) % count if i % 2 else (i - 1) % count) for i in range(count)]

    up = [(i, (i + 1) % 4) for i in range(4)]
    swap = [(0, 1), (1, 0)]
    za = lax.ppermute(za, "zhi", swap)
    zb = lax.ppermute(zb, gz, cross(8))
    inner = lax.ppermute(inner, "core", swap)
    outer = lax.ppermute(outer, gy, cross(16))
    xlow = lax.ppermute(xs, gx, up)
    xhigh = lax.ppermute(xs, gx, [(target, source) for source, target in up])
    base = along_z(place, y, vel, za, zb)
    updated = along_xy(place, y, vel, base, outer, inner, xlow, xhigh, *x_matrices(width))

    lines = exchange(updated.reshape(4, species * rows * depth // 4, width), gx)
    mine, other = gram_blocks(place, lines)
    mine = mine + lax.ppermute(other, "core", swap)
    plane = ("gx", "x")
    part = jnp.sum(exchange(mine.reshape(16, -1, 128), plane), axis=0)
    part = gather_sum(part, ("znear",), 4)
    part = gather_sum(part, ("zpair", "zhi"), 4)
    mine = exchange(jnp.broadcast_to(part, (16,) + part.shape), plane).reshape(-1, 128)
    other = lax.ppermute(mine, "core", swap)
    cells = species * rows * 16 * depth * 8
    return updated, gram_rows(place, mine, other, 1.0 / cells)


def solution(mesh):
    axes = ("gx", "zpair", "znear", "core", "x", "zhi")
    fine = Mesh(mesh.devices.reshape(4, 2, 4, 2, 4, 2), axes)
    grid = P(None, ("zpair", "znear", "core"), ("x", "zhi"), "gx")
    return jax.shard_map(
        shards, mesh=fine, in_specs=(grid, grid), out_specs=(grid, P("gx", None)), check_vma=False
    )
```

```python
import functools

import ml_dtypes
import numpy as np
import jax
import jax.numpy as jnp
from jax import lax
from jax.experimental import pallas as pl
from jax.experimental.pallas import tpu as pltpu
from jax.sharding import Mesh, PartitionSpec as P

C1 = (4.0 / 5.0, -1.0 / 5.0, 4.0 / 105.0, -1.0 / 280.0)
C2 = (-205.0 / 72.0, 8.0 / 5.0, -1.0 / 5.0, 8.0 / 315.0, -1.0 / 560.0)
DIFF = (0.10, 0.12, 0.08, 0.15)
NU = (-1.0, -1.0, 2.0, 0.0)
PAIRS = [(a, b) for a in range(4) for b in range(a, 4)]
MIB = 1 << 20


def split(value):
    high = value.astype(jnp.bfloat16)
    return high, (value - high.astype(jnp.float32)).astype(jnp.bfloat16)


def x_matrices(width):
    matrix = np.zeros((2 * width, 2 * width))
    for i in range(width):
        for k in range(-4, 5):
            j = i + k
            row = j if 0 <= j < width else (width + 4 + j if j < 0 else width + 4 + j - width)
            if k:
                matrix[row, i] += np.sign(k) * C1[abs(k) - 1]
            matrix[row, width + i] += C2[abs(k)]
    matrix = matrix.astype(np.float32)
    high = matrix.astype(ml_dtypes.bfloat16)
    return high, (matrix - high.astype(np.float32)).astype(ml_dtypes.bfloat16)


def dot(left, right):
    return lax.dot_general(
        left, right, (((1,), (0,)), ((), ())), preferred_element_type=jnp.float32
    )


def lanes():
    return lax.broadcasted_iota(jnp.int32, (8, 128), 1)


def pack_body(place, y, inner, outer, za, zb, xs):
    count, rows, depth, width = y.shape
    core, half = place[1], place[2]
    lane = lanes()

    def species(s, carry):
        inner[s] = y[s, pl.ds(4 * (1 - core), 4)]
        outer[s] = y[s, pl.ds(4 * core, 4)]
        for j in range(rows):
            low, high = y[s, j, 0:4], y[s, j, depth - 4 :]
            at = 4 * (j % 2)
            za[s, j // 2, at : at + 4] = jnp.where(half == 0, high, low)
            zb[s, j // 2, at : at + 4] = jnp.where(half == 0, low, high)
            packed = jnp.zeros((8, width), jnp.float32)
            for g in range(depth // 8):
                turned = pltpu.roll(y[s, j, 8 * g : 8 * g + 8], 8 * g + 4, 1)
                packed = jnp.where(lane // 8 == g, turned, packed)
            xs[s, j] = packed
        return carry

    lax.fori_loop(0, count, species, 0)


SMEM = pl.BlockSpec(memory_space=pltpu.SMEM)
VMEM = pl.BlockSpec(memory_space=pltpu.VMEM)


def pack(place, y):
    count, rows, depth, width = y.shape
    shapes = [(count, 4, depth, width)] * 2 + [(count, rows // 2, 8, width)] * 2
    shapes = shapes + [(count, rows, 8, width)]
    return pl.pallas_call(
        pack_body,
        out_shape=[jax.ShapeDtypeStruct(shape, jnp.float32) for shape in shapes],
        in_specs=[SMEM, VMEM],
        out_specs=[VMEM] * 5,
        compiler_params=pltpu.CompilerParams(vmem_limit_bytes=24 * MIB),
        name="pack",
    )(place, y)


def factors(s, count):
    diff = jnp.float32(0.25 * DIFF[0])
    nu = jnp.float32(NU[0])
    for q in range(1, count):
        diff = jnp.where(s == q, jnp.float32(0.25 * DIFF[q]), diff)
        nu = jnp.where(s == q, jnp.float32(NU[q]), nu)
    return diff, nu


def layers_body(front, place, y, vel, face, zs, xlow, xhigh, mh, ml, out, side, dx, pad):
    count, rows, depth, width = y.shape
    ahead_of = place[1] == front
    start = jnp.where(ahead_of, 0, 4)
    below = lanes() % 8 < 4
    spot = pl.ds(8, depth)

    def species(s, carry):
        diff, nu = factors(s, count)
        pad[pl.ds(4 - start, rows), spot] = y[s]
        pad[pl.ds(2 * start, 4), spot] = face[s]
        for i in range(4):
            at = 4 * (i % 2)
            tile = start // 2 + i // 2
            pad[4 + i, 4:8] = zs[0, s, tile, at : at + 4]
            pad[4 + i, 8 + depth : 12 + depth] = zs[1, s, tile, at : at + 4]
            packed = jnp.where(below, xlow[s, start + i], xhigh[s, start + i])
            for g in range(depth // 8):
                row = i * depth + 8 * g
                side[row : row + 8] = pltpu.roll(packed, (128 - 8 * g) % 128, 1)
        own = y[s, pl.ds(start, 4)].reshape(4 * depth, width)
        high, low = split(jnp.concatenate([own, side[...]], axis=1))
        dx[...] = dot(high, mh[...]) + (dot(low, mh[...]) + dot(high, ml[...]))
        for i in range(4):
            centre = y[s, start + i]
            d1y = d1z = None
            second = (2.0 * C2[0]) * centre + dx[i * depth : (i + 1) * depth, width:]
            for k in range(1, 5):
                ya, yb = pad[4 + i + k, 8 : 8 + depth], pad[4 + i - k, 8 : 8 + depth]
                na, nb = pad[4 + i, 8 + k : 8 + k + depth], pad[4 + i, 8 - k : 8 - k + depth]
                ty, tz = (0.25 * C1[k - 1]) * (ya - yb), (0.25 * C1[k - 1]) * (na - nb)
                d1y = ty if d1y is None else d1y + ty
                d1z = tz if d1z is None else d1z + tz
                second = second + C2[k] * ((ya + yb) + (na + nb))
            moved = (0.25 * vel[0, start + i]) * dx[i * depth : (i + 1) * depth, :width]
            moved = moved + (vel[1, start + i] * d1y + vel[2, start + i] * d1z)
            heat = 1.0 + 3.0 * y[2, start + i]
            rate = y[0, start + i] * y[1, start + i] * jnp.exp(-3.0 / heat)
            out[s, i] = centre + (diff * second - moved + nu * rate)
        return carry

    lax.fori_loop(0, count, species, 0)


def layers(front, place, y, *rest):
    count, rows, depth, width = y.shape
    return pl.pallas_call(
        functools.partial(layers_body, front),
        out_shape=jax.ShapeDtypeStruct((count, 4, depth, width), jnp.float32),
        in_specs=[SMEM] + [VMEM] * (1 + len(rest)),
        out_specs=VMEM,
        scratch_shapes=[
            pltpu.VMEM((4 * depth, width), jnp.float32),
            pltpu.VMEM((4 * depth, 2 * width), jnp.float32),
            pltpu.VMEM((12, depth + 16, width), jnp.float32),
        ],
        compiler_params=pltpu.CompilerParams(vmem_limit_bytes=24 * MIB),
        cost_estimate=pl.CostEstimate(
            flops=10**8, bytes_accessed=6 * 10**6, transcendentals=0
        ),
        name="layers",
    )(place, y, *rest)


def z_faces_body(place, za, zb, out):
    out[0] = jnp.where(place[2] == 0, zb[...], za[...])
    out[1] = jnp.where(place[2] == 0, za[...], zb[...])


def z_faces(place, za, zb):
    return pl.pallas_call(
        z_faces_body,
        out_shape=jax.ShapeDtypeStruct((2,) + za.shape, jnp.float32),
        in_specs=[SMEM, VMEM, VMEM],
        out_specs=VMEM,
        cost_estimate=pl.CostEstimate(
            flops=18 * 10**8, bytes_accessed=10**7, transcendentals=0
        ),
        name="z_faces",
    )(place, za, zb)


def join_body(place, inner, outer, out):
    core = place[1]
    out[:, pl.ds(4 - 4 * core, 4)] = inner[...]
    out[:, pl.ds(4 * core, 4)] = outer[...]


def join(place, inner, outer):
    count, rows, depth, width = inner.shape
    return pl.pallas_call(
        join_body,
        out_shape=jax.ShapeDtypeStruct((count, 2 * rows, depth, width), jnp.float32),
        in_specs=[SMEM, VMEM, VMEM],
        out_specs=VMEM,
        compiler_params=pltpu.CompilerParams(vmem_limit_bytes=24 * MIB),
        name="join",
    )(place, inner, outer)


def gram_body(place, lines, *rest):
    *before, mine, other = rest
    parts = lines.shape[0]
    whole = jnp.concatenate([lines[a] for a in range(parts)], axis=1)
    high, low = split(whole)
    turned_high, turned_low = split(whole.T)
    total = dot(turned_high, high) + (dot(turned_high, low) + dot(turned_low, high))
    tiles = [total[a * 128 : (a + 1) * 128, b * 128 : (b + 1) * 128] for a, b in PAIRS]
    for q in range(5):
        at = slice(q * 128, (q + 1) * 128)
        first = jnp.where(place[1] == 0, tiles[q], tiles[q + 5])
        second = jnp.where(place[1] == 0, tiles[q + 5], tiles[q])
        if before:
            first, second = first + before[0][at], second + before[1][at]
        mine[at] = first
        other[at] = second


def gram_blocks(place, lines, *before):
    return pl.pallas_call(
        gram_body,
        out_shape=[jax.ShapeDtypeStruct((len(PAIRS) * 64, 128), jnp.float32)] * 2,
        in_specs=[SMEM] + [VMEM] * (1 + len(before)),
        out_specs=[VMEM] * 2,
        compiler_params=pltpu.CompilerParams(vmem_limit_bytes=32 * MIB),
        name="gram",
    )(place, lines, *before)


def rows_body(scale, place, mine, other, out):
    row, core = place[0], place[1]
    for b in range(4):
        low, top = jnp.minimum(row, b), jnp.maximum(row, b)
        index = low * 4 - (low * (low - 1)) // 2 + (top - low)
        owner = jnp.where(index >= 5, 1, 0)
        at = pl.ds(pl.multiple_of((index - 5 * owner) * 128, 128), 128)
        tile = jnp.where(owner == core, mine[at], other[at]) * scale
        out[:, b * 128 : (b + 1) * 128] = jnp.where(row <= b, tile, tile.T)


def gram_rows(place, mine, other, scale):
    return pl.pallas_call(
        functools.partial(rows_body, scale),
        out_shape=jax.ShapeDtypeStruct((128, 512), jnp.float32),
        in_specs=[SMEM, VMEM, VMEM],
        out_specs=VMEM,
        name="gram_rows",
    )(place, mine, other)


def exchange(pieces, axes):
    return lax.all_to_all(pieces, axes, split_axis=0, concat_axis=0, tiled=True)


def gather_sum(part, axes, count):
    return jnp.sum(exchange(jnp.broadcast_to(part, (count,) + part.shape), axes), axis=0)


def shards(y, vel):
    species, rows, depth, width = y.shape
    gy, gz, gx = ("zpair", "znear", "core"), ("x", "zhi"), ("gx",)
    place = jnp.stack([lax.axis_index("gx"), lax.axis_index("core"), lax.axis_index("zhi")])
    place = place.astype(jnp.int32)
    inner, outer, za, zb, xs = pack(place, y)

    def cross(count):
        return [(i, (i + 1) % count if i % 2 else (i - 1) % count) for i in range(count)]

    up = [(i, (i + 1) % 4) for i in range(4)]
    swap = [(0, 1), (1, 0)]
    za = lax.ppermute(za, "zhi", swap)
    zb = lax.ppermute(zb, gz, cross(8))
    inner = lax.ppermute(inner, "core", swap)
    outer = lax.ppermute(outer, gy, cross(16))
    xlow = lax.ppermute(xs, gx, up)
    xhigh = lax.ppermute(xs, gx, [(target, source) for source, target in up])
    rest = (z_faces(place, za, zb), xlow, xhigh) + x_matrices(width)
    near = layers(1, place, y, vel, inner, *rest)
    pieces = (4, species * depth, width)
    sums = gram_blocks(place, exchange(near.reshape(pieces), gx))
    far = layers(0, place, y, vel, outer, *rest)
    mine, other = gram_blocks(place, exchange(far.reshape(pieces), gx), *sums)
    updated = join(place, near, far)
    mine = mine + lax.ppermute(other, "core", swap)
    plane = ("gx", "x")
    part = jnp.sum(exchange(mine.reshape(16, -1, 128), plane), axis=0)
    part = gather_sum(part, ("znear",), 4)
    part = gather_sum(part, ("zpair", "zhi"), 4)
    mine = exchange(jnp.broadcast_to(part, (16,) + part.shape), plane).reshape(-1, 128)
    other = lax.ppermute(mine, "core", swap)
    cells = species * rows * 16 * depth * 8
    return updated, gram_rows(place, mine, other, 1.0 / cells)


def solution(mesh):
    axes = ("gx", "zpair", "znear", "core", "x", "zhi")
    fine = Mesh(mesh.devices.reshape(4, 2, 4, 2, 4, 2), axes)
    grid = P(None, ("zpair", "znear", "core"), ("x", "zhi"), "gx")
    return jax.shard_map(
        shards, mesh=fine, in_specs=(grid, grid), out_specs=(grid, P("gx", None)), check_vma=False
    )
```

```python
import functools

import jax
import jax.numpy as jnp
from jax import lax
from jax.experimental import pallas as pl
from jax.experimental.pallas import tpu as pltpu
from jax.sharding import Mesh, PartitionSpec as P

C1 = (4.0 / 5.0, -1.0 / 5.0, 4.0 / 105.0, -1.0 / 280.0)
C2 = (-205.0 / 72.0, 8.0 / 5.0, -1.0 / 5.0, 8.0 / 315.0, -1.0 / 560.0)
DIFF = (0.10, 0.12, 0.08, 0.15)
NU = (-1.0, -1.0, 2.0, 0.0)
PAIRS = [(a, b) for a in range(4) for b in range(a, 4)]
MIB = 1 << 20


def split(value):
    high = value.astype(jnp.bfloat16)
    return high, (value - high.astype(jnp.float32)).astype(jnp.bfloat16)


def x_matrices(width):
    row = lax.broadcasted_iota(jnp.int32, (2 * width, width), 0)
    cell = jnp.where(row < width, row, jnp.where(row < width + 4, row - width - 4, row - 4))
    cell = jnp.where(row < width + 8, cell, 4 * width)
    step = cell - lax.broadcasted_iota(jnp.int32, (2 * width, width), 1)
    first = jnp.zeros((2 * width, width), jnp.float32)
    second = jnp.where(step == 0, jnp.float32(C2[0]), first)
    for k in range(1, 5):
        first = jnp.where(step == k, jnp.float32(C1[k - 1]), first)
        first = jnp.where(step == -k, jnp.float32(-C1[k - 1]), first)
        second = jnp.where(jnp.abs(step) == k, jnp.float32(C2[k]), second)
    return jnp.concatenate([first, second], axis=1)


def dot(left, right):
    return lax.dot_general(
        left, right, (((1,), (0,)), ((), ())), preferred_element_type=jnp.float32
    )


def lanes():
    return lax.broadcasted_iota(jnp.int32, (8, 128), 1)


def pack_body(y, inner, outer, za, zb, xs):
    count, rows, depth, width = y.shape
    core, half = lax.axis_index("core"), lax.axis_index("zhi")
    lane = lanes()

    def species(s, carry):
        inner[s] = y[s, pl.ds(4 * (1 - core), 4)]
        outer[s] = y[s, pl.ds(4 * core, 4)]
        for j in range(rows):
            low, high = y[s, j, 0:4], y[s, j, depth - 4 :]
            at = 4 * (j % 2)
            za[s, j // 2, at : at + 4] = jnp.where(half == 0, high, low)
            zb[s, j // 2, at : at + 4] = jnp.where(half == 0, low, high)
            packed = jnp.zeros((8, width), jnp.float32)
            for g in range(depth // 8):
                turned = pltpu.roll(y[s, j, 8 * g : 8 * g + 8], 8 * g + 4, 1)
                packed = jnp.where(lane // 8 == g, turned, packed)
            xs[s, j] = packed
        return carry

    lax.fori_loop(0, count, species, 0)


VMEM = pl.BlockSpec(memory_space=pltpu.VMEM)


def pack(y):
    count, rows, depth, width = y.shape
    shapes = [(count, 4, depth, width)] * 2 + [(count, rows // 2, 8, width)] * 2
    shapes = shapes + [(count, rows, 8, width)]
    return pl.pallas_call(
        pack_body,
        out_shape=[jax.ShapeDtypeStruct(shape, jnp.float32) for shape in shapes],
        in_specs=[VMEM],
        out_specs=[VMEM] * 5,
        compiler_params=pltpu.CompilerParams(vmem_limit_bytes=24 * MIB),
        name="pack",
    )(y)


def factors(s, count):
    diff = jnp.float32(0.25 * DIFF[0])
    nu = jnp.float32(NU[0])
    for q in range(1, count):
        diff = jnp.where(s == q, jnp.float32(0.25 * DIFF[q]), diff)
        nu = jnp.where(s == q, jnp.float32(NU[q]), nu)
    return diff, nu


def layers_body(front, y, vel, face, zs, xlow, xhigh, out, side, dx, pad, rate, zbuf, mh, ml, sem):
    count, rows, depth, width = y.shape
    load = pltpu.make_async_copy(zs, zbuf, sem)
    load.start()
    start = jnp.where(lax.axis_index("core") == front, 0, 4)
    below = lanes() % 8 < 4
    spot = pl.ds(8, depth)
    mh[...], ml[...] = split(x_matrices(width))
    for i in range(4):
        heat = 1.0 + 3.0 * y[2, start + i]
        rate[i] = y[0, start + i] * y[1, start + i] * jnp.exp(-3.0 / heat)
    load.wait()

    def species(s, carry):
        diff, nu = factors(s, count)
        pad[pl.ds(4 - start, rows), spot] = y[s]
        pad[pl.ds(2 * start, 4), spot] = face[s]
        for i in range(4):
            at = 4 * (i % 2)
            tile = start // 2 + i // 2
            pad[4 + i, 4:8] = zbuf[0, s, tile, at : at + 4]
            pad[4 + i, 8 + depth : 12 + depth] = zbuf[1, s, tile, at : at + 4]
            packed = jnp.where(below, xlow[s, start + i], xhigh[s, start + i])
            for g in range(depth // 8):
                row = i * depth + 8 * g
                side[row : row + 8] = pltpu.roll(packed, (128 - 8 * g) % 128, 1)
        own = y[s, pl.ds(start, 4)].reshape(4 * depth, width)
        high, low = split(jnp.concatenate([own, side[...]], axis=1))
        dx[...] = dot(high, mh[...]) + (dot(low, mh[...]) + dot(high, ml[...]))
        for i in range(4):
            centre = y[s, start + i]
            d1y = d1z = None
            second = (2.0 * C2[0]) * centre + dx[i * depth : (i + 1) * depth, width:]
            for k in range(1, 5):
                ya, yb = pad[4 + i + k, 8 : 8 + depth], pad[4 + i - k, 8 : 8 + depth]
                na, nb = pad[4 + i, 8 + k : 8 + k + depth], pad[4 + i, 8 - k : 8 - k + depth]
                ty, tz = (0.25 * C1[k - 1]) * (ya - yb), (0.25 * C1[k - 1]) * (na - nb)
                d1y = ty if d1y is None else d1y + ty
                d1z = tz if d1z is None else d1z + tz
                second = second + C2[k] * ((ya + yb) + (na + nb))
            moved = (0.25 * vel[0, start + i]) * dx[i * depth : (i + 1) * depth, :width]
            moved = moved + (vel[1, start + i] * d1y + vel[2, start + i] * d1z)
            out[s, i] = centre + (diff * second - moved + nu * rate[i])
        return carry

    lax.fori_loop(0, count, species, 0)


def layers(front, y, vel, face, zs, *rest):
    count, rows, depth, width = y.shape
    return pl.pallas_call(
        functools.partial(layers_body, front),
        out_shape=jax.ShapeDtypeStruct((count, 4, depth, width), jnp.float32),
        in_specs=[VMEM] * 3 + [pl.BlockSpec(memory_space=pltpu.HBM)] + [VMEM] * len(rest),
        out_specs=VMEM,
        scratch_shapes=[
            pltpu.VMEM((4 * depth, width), jnp.float32),
            pltpu.VMEM((4 * depth, 2 * width), jnp.float32),
            pltpu.VMEM((12, depth + 16, width), jnp.float32),
            pltpu.VMEM((4, depth, width), jnp.float32),
            pltpu.VMEM(zs.shape, jnp.float32),
            pltpu.VMEM((2 * width, 2 * width), jnp.bfloat16),
            pltpu.VMEM((2 * width, 2 * width), jnp.bfloat16),
            pltpu.SemaphoreType.DMA,
        ],
        compiler_params=pltpu.CompilerParams(vmem_limit_bytes=24 * MIB),
        cost_estimate=pl.CostEstimate(
            flops=10**8, bytes_accessed=6 * 10**6, transcendentals=0
        ),
        name="layers",
    )(y, vel, face, zs, *rest)


def z_faces_body(za, zb, out):
    half = lax.axis_index("zhi")
    out[0] = jnp.where(half == 0, zb[...], za[...])
    out[1] = jnp.where(half == 0, za[...], zb[...])


def z_faces(za, zb):
    return pl.pallas_call(
        z_faces_body,
        out_shape=jax.ShapeDtypeStruct((2,) + za.shape, jnp.float32),
        in_specs=[VMEM, VMEM],
        out_specs=VMEM,
        cost_estimate=pl.CostEstimate(
            flops=18 * 10**8, bytes_accessed=10**7, transcendentals=0
        ),
        name="z_faces",
    )(za, zb)


def products(lines):
    whole = jnp.concatenate([lines[a] for a in range(lines.shape[0])], axis=1)
    high, low = split(whole)
    turned_high, turned_low = split(whole.T)
    total = dot(turned_high, high) + (dot(turned_high, low) + dot(turned_low, high))
    return [total[a * 128 : (a + 1) * 128, b * 128 : (b + 1) * 128] for a, b in PAIRS]


def first_body(lines, inner, outer, sums, updated):
    core = lax.axis_index("core")
    for q, tile in enumerate(products(lines)):
        sums[q * 128 : (q + 1) * 128] = tile
    updated[:, pl.ds(4 - 4 * core, 4)] = inner[...]
    updated[:, pl.ds(4 * core, 4)] = outer[...]


def first_half(lines, inner, outer):
    count, rows, depth, width = inner.shape
    return pl.pallas_call(
        first_body,
        out_shape=[
            jax.ShapeDtypeStruct((len(PAIRS) * 128, 128), jnp.float32),
            jax.ShapeDtypeStruct((count, 2 * rows, depth, width), jnp.float32),
        ],
        in_specs=[VMEM] * 3,
        out_specs=[VMEM] * 2,
        compiler_params=pltpu.CompilerParams(vmem_limit_bytes=32 * MIB),
        name="first_half",
    )(lines, inner, outer)


def second_body(lines, sums, mine, other):
    core = lax.axis_index("core")
    tiles = products(lines)
    for q in range(5):
        at = slice(q * 128, (q + 1) * 128)
        low = tiles[q] + sums[at]
        high = tiles[q + 5] + sums[(q + 5) * 128 : (q + 6) * 128]
        mine[at] = jnp.where(core == 0, low, high)
        other[at] = jnp.where(core == 0, high, low)


def second_half(lines, sums):
    return pl.pallas_call(
        second_body,
        out_shape=[jax.ShapeDtypeStruct((len(PAIRS) * 64, 128), jnp.float32)] * 2,
        in_specs=[VMEM] * 2,
        out_specs=[VMEM] * 2,
        compiler_params=pltpu.CompilerParams(vmem_limit_bytes=32 * MIB),
        name="second_half",
    )(lines, sums)


def rows_body(scale, mine, other, out):
    row, core = lax.axis_index("gx"), lax.axis_index("core")
    for b in range(4):
        low, top = jnp.minimum(row, b), jnp.maximum(row, b)
        index = low * 4 - (low * (low - 1)) // 2 + (top - low)
        owner = jnp.where(index >= 5, 1, 0)
        at = pl.ds(pl.multiple_of((index - 5 * owner) * 128, 128), 128)
        tile = jnp.where(owner == core, mine[at], other[at]) * scale
        out[:, b * 128 : (b + 1) * 128] = jnp.where(row <= b, tile, tile.T)


def gram_rows(mine, other, scale):
    return pl.pallas_call(
        functools.partial(rows_body, scale),
        out_shape=jax.ShapeDtypeStruct((128, 512), jnp.float32),
        in_specs=[VMEM, VMEM],
        out_specs=VMEM,
        name="gram_rows",
    )(mine, other)


def exchange(pieces, axes):
    return lax.all_to_all(pieces, axes, split_axis=0, concat_axis=0, tiled=True)


def gather_sum(part, axes, count):
    return jnp.sum(exchange(jnp.broadcast_to(part, (count,) + part.shape), axes), axis=0)


def shards(y, vel):
    species, rows, depth, width = y.shape
    gy, gz, gx = ("zpair", "znear", "core"), ("x", "zhi"), ("gx",)
    inner, outer, za, zb, xs = pack(y)

    def cross(count):
        return [(i, (i + 1) % count if i % 2 else (i - 1) % count) for i in range(count)]

    up = [(i, (i + 1) % 4) for i in range(4)]
    swap = [(0, 1), (1, 0)]
    za = lax.ppermute(za, "zhi", swap)
    zb = lax.ppermute(zb, gz, cross(8))
    inner = lax.ppermute(inner, "core", swap)
    outer = lax.ppermute(outer, gy, cross(16))
    xlow = lax.ppermute(xs, gx, up)
    xhigh = lax.ppermute(xs, gx, [(target, source) for source, target in up])
    rest = (z_faces(za, zb), xlow, xhigh)
    pieces = (4, species * depth, width)
    near = layers(1, y, vel, inner, *rest)
    far = layers(0, y, vel, outer, *rest)
    sums, updated = first_half(exchange(near.reshape(pieces), gx), near, far)
    mine, other = second_half(exchange(far.reshape(pieces), gx), sums)
    mine = mine + lax.ppermute(other, "core", swap)
    plane = ("gx", "x")
    part = jnp.sum(exchange(mine.reshape(16, -1, 128), plane), axis=0)
    part = gather_sum(part, ("znear",), 4)
    part = gather_sum(part, ("zpair", "zhi"), 4)
    mine = exchange(jnp.broadcast_to(part, (16,) + part.shape), plane).reshape(-1, 128)
    other = lax.ppermute(mine, "core", swap)
    cells = species * rows * 16 * depth * 8
    return updated, gram_rows(mine, other, 1.0 / cells)


def solution(mesh):
    axes = ("gx", "zpair", "znear", "core", "x", "zhi")
    fine = Mesh(mesh.devices.reshape(4, 2, 4, 2, 4, 2), axes)
    grid = P(None, ("zpair", "znear", "core"), ("x", "zhi"), "gx")
    return jax.shard_map(
        shards, mesh=fine, in_specs=(grid, grid), out_specs=(grid, P("gx", None)), check_vma=False
    )
```

```python
import functools

import jax
import jax.numpy as jnp
from jax import lax
from jax.experimental import pallas as pl
from jax.experimental.pallas import tpu as pltpu
from jax.sharding import Mesh, PartitionSpec as P

C1 = (4.0 / 5.0, -1.0 / 5.0, 4.0 / 105.0, -1.0 / 280.0)
C2 = (-205.0 / 72.0, 8.0 / 5.0, -1.0 / 5.0, 8.0 / 315.0, -1.0 / 560.0)
DIFF = (0.10, 0.12, 0.08, 0.15)
NU = (-1.0, -1.0, 2.0, 0.0)
PAIRS = [(a, b) for a in range(4) for b in range(a, 4)]
MIB = 1 << 20


def split(value):
    high = value.astype(jnp.bfloat16)
    return high, (value - high.astype(jnp.float32)).astype(jnp.bfloat16)


def x_matrices(width):
    row = lax.broadcasted_iota(jnp.int32, (2 * width, width), 0)
    cell = jnp.where(row < width, row, jnp.where(row < width + 4, row - width - 4, row - 4))
    cell = jnp.where(row < width + 8, cell, 4 * width)
    step = cell - lax.broadcasted_iota(jnp.int32, (2 * width, width), 1)
    first = jnp.zeros((2 * width, width), jnp.float32)
    second = jnp.where(step == 0, jnp.float32(C2[0]), first)
    for k in range(1, 5):
        first = jnp.where(step == k, jnp.float32(C1[k - 1]), first)
        first = jnp.where(step == -k, jnp.float32(-C1[k - 1]), first)
        second = jnp.where(jnp.abs(step) == k, jnp.float32(C2[k]), second)
    return jnp.concatenate([first, second], axis=1)


def dot(left, right):
    return lax.dot_general(
        left, right, (((1,), (0,)), ((), ())), preferred_element_type=jnp.float32
    )


def lanes():
    return lax.broadcasted_iota(jnp.int32, (8, 128), 1)


def pack_body(y, inner, outer, za, zb, xs):
    count, rows, depth, width = y.shape
    core, half = lax.axis_index("core"), lax.axis_index("zhi")
    lane = lanes()

    def species(s, carry):
        inner[s] = y[s, pl.ds(4 * (1 - core), 4)]
        outer[s] = y[s, pl.ds(4 * core, 4)]
        for j in range(rows):
            low, high = y[s, j, 0:4], y[s, j, depth - 4 :]
            at = 4 * (j % 2)
            za[s, j // 2, at : at + 4] = jnp.where(half == 0, high, low)
            zb[s, j // 2, at : at + 4] = jnp.where(half == 0, low, high)
            packed = jnp.zeros((8, width), jnp.float32)
            for g in range(depth // 8):
                turned = pltpu.roll(y[s, j, 8 * g : 8 * g + 8], 8 * g + 4, 1)
                packed = jnp.where(lane // 8 == g, turned, packed)
            xs[s, j] = packed
        return carry

    lax.fori_loop(0, count, species, 0)


VMEM = pl.BlockSpec(memory_space=pltpu.VMEM)


def pack(y):
    count, rows, depth, width = y.shape
    shapes = [(count, 4, depth, width)] * 2 + [(count, rows // 2, 8, width)] * 2
    shapes = shapes + [(count, rows, 8, width)]
    return pl.pallas_call(
        pack_body,
        out_shape=[jax.ShapeDtypeStruct(shape, jnp.float32) for shape in shapes],
        in_specs=[VMEM],
        out_specs=[VMEM] * 5,
        compiler_params=pltpu.CompilerParams(vmem_limit_bytes=24 * MIB),
        name="pack",
    )(y)


def factors(s, count):
    diff = jnp.float32(0.25 * DIFF[0])
    nu = jnp.float32(NU[0])
    for q in range(1, count):
        diff = jnp.where(s == q, jnp.float32(0.25 * DIFF[q]), diff)
        nu = jnp.where(s == q, jnp.float32(NU[q]), nu)
    return diff, nu


def along_z_body(y, vel, za, zb, out, rate, pad):
    count, rows, depth, width = y.shape
    half = lax.axis_index("zhi")
    for j in range(rows):
        heat = 1.0 + 3.0 * y[2, j]
        rate[j] = y[0, j] * y[1, j] * jnp.exp(-3.0 / heat)

    def species(s, carry):
        diff, nu = factors(s, count)
        for j in range(rows):
            at = 4 * (j % 2)
            fa, fb = za[s, j // 2, at : at + 4], zb[s, j // 2, at : at + 4]
            pad[j, 4:8] = jnp.where(half == 0, fb, fa)
            pad[j, 8 : 8 + depth] = y[s, j]
            pad[j, 8 + depth : 12 + depth] = jnp.where(half == 0, fa, fb)
        for j in range(rows):
            centre = y[s, j]
            first = None
            second = (2.0 * C2[0]) * centre
            for k in range(1, 5):
                ahead, behind = pad[j, 8 + k : 8 + k + depth], pad[j, 8 - k : 8 - k + depth]
                term = (0.25 * C1[k - 1]) * (ahead - behind)
                first = term if first is None else first + term
                second = second + C2[k] * (ahead + behind)
            out[s, j] = centre + (diff * second - vel[2, j] * first + nu * rate[j])
        return carry

    lax.fori_loop(0, count, species, 0)


def along_z(y, *rest):
    _, rows, depth, width = y.shape
    return pl.pallas_call(
        along_z_body,
        out_shape=jax.ShapeDtypeStruct(y.shape, jnp.float32),
        in_specs=[VMEM] * (1 + len(rest)),
        out_specs=VMEM,
        scratch_shapes=[
            pltpu.VMEM((rows, depth, width), jnp.float32),
            pltpu.VMEM((rows, depth + 16, width), jnp.float32),
        ],
        compiler_params=pltpu.CompilerParams(vmem_limit_bytes=24 * MIB),
        cost_estimate=pl.CostEstimate(
            flops=10**9, bytes_accessed=10**7, transcendentals=0
        ),
        name="along_z",
    )(y, *rest)


def along_xy_body(y, vel, base, outer, inner, xlow, xhigh, out, side, dx, pad):
    count, rows, depth, width = y.shape
    core = lax.axis_index("core")
    below = lanes() % 8 < 4
    mh, ml = split(x_matrices(width))

    def species(s, carry):
        diff, _ = factors(s, count)
        pad[pl.ds(12 * (1 - core), 4)] = inner[s]
        pad[pl.ds(12 * core, 4)] = outer[s]
        pad[4 : 4 + rows] = y[s]
        for j in range(rows):
            packed = jnp.where(below, xlow[s, j], xhigh[s, j])
            for g in range(depth // 8):
                row = j * depth + 8 * g
                side[row : row + 8] = pltpu.roll(packed, (128 - 8 * g) % 128, 1)
        left = jnp.concatenate([y[s].reshape(rows * depth, width), side[...]], axis=1)
        high, low = split(left)
        dx[...] = dot(high, mh) + (dot(low, mh) + dot(high, ml))
        for j in range(rows):
            first = None
            second = dx[j * depth : (j + 1) * depth, width:]
            for k in range(1, 5):
                ahead, behind = pad[4 + j + k], pad[4 + j - k]
                term = (0.25 * C1[k - 1]) * (ahead - behind)
                first = term if first is None else first + term
                second = second + C2[k] * (ahead + behind)
            moved = (0.25 * vel[0, j]) * dx[j * depth : (j + 1) * depth, :width]
            out[s, j] = base[s, j] + (diff * second - (moved + vel[1, j] * first))
        return carry

    lax.fori_loop(0, count, species, 0)


def along_xy(y, *rest):
    _, rows, depth, width = y.shape
    return pl.pallas_call(
        along_xy_body,
        out_shape=jax.ShapeDtypeStruct(y.shape, jnp.float32),
        in_specs=[VMEM] * (1 + len(rest)),
        out_specs=VMEM,
        scratch_shapes=[
            pltpu.VMEM((rows * depth, width), jnp.float32),
            pltpu.VMEM((rows * depth, 2 * width), jnp.float32),
            pltpu.VMEM((rows + 8, depth, width), jnp.float32),
        ],
        compiler_params=pltpu.CompilerParams(vmem_limit_bytes=32 * MIB),
        name="along_xy",
    )(y, *rest)


def products(lines):
    whole = jnp.concatenate([lines[a] for a in range(lines.shape[0])], axis=1)
    high, low = split(whole)
    turned_high, turned_low = split(whole.T)
    total = dot(turned_high, high) + (dot(turned_high, low) + dot(turned_low, high))
    return [total[a * 128 : (a + 1) * 128, b * 128 : (b + 1) * 128] for a, b in PAIRS]


def gram_body(lines, mine, other):
    core = lax.axis_index("core")
    tiles = products(lines)
    for q in range(5):
        at = slice(q * 128, (q + 1) * 128)
        mine[at] = jnp.where(core == 0, tiles[q], tiles[q + 5])
        other[at] = jnp.where(core == 0, tiles[q + 5], tiles[q])


def gram_blocks(lines):
    return pl.pallas_call(
        gram_body,
        out_shape=[jax.ShapeDtypeStruct((len(PAIRS) * 64, 128), jnp.float32)] * 2,
        in_specs=[VMEM],
        out_specs=[VMEM] * 2,
        compiler_params=pltpu.CompilerParams(vmem_limit_bytes=40 * MIB),
        name="gram",
    )(lines)


def rows_body(scale, mine, other, out, tiles, sems):
    row, core = lax.axis_index("gx"), lax.axis_index("core")

    def tile(b):
        low, top = jnp.minimum(row, b), jnp.maximum(row, b)
        index = low * 4 - (low * (low - 1)) // 2 + (top - low)
        owner = jnp.where(index >= 5, 1, 0)
        at = pl.ds(pl.multiple_of((index - 5 * owner) * 128, 128), 128)
        return owner == core, at

    for b in range(4):
        here, at = tile(b)

        @pl.when(here)
        def _():
            pltpu.make_async_copy(mine.at[at], tiles.at[b], sems.at[b]).start()

        @pl.when(jnp.logical_not(here))
        def _():
            pltpu.make_async_copy(other.at[at], tiles.at[b], sems.at[b]).start()

    for b in range(4):
        pltpu.make_async_copy(mine.at[pl.ds(0, 128)], tiles.at[b], sems.at[b]).wait()
        block = tiles[b] * scale
        out[:, b * 128 : (b + 1) * 128] = jnp.where(row <= b, block, block.T)


def gram_rows(mine, other, scale):
    return pl.pallas_call(
        functools.partial(rows_body, scale),
        out_shape=jax.ShapeDtypeStruct((128, 512), jnp.float32),
        in_specs=[pl.BlockSpec(memory_space=pl.ANY)] * 2,
        out_specs=VMEM,
        scratch_shapes=[
            pltpu.VMEM((4, 128, 128), jnp.float32),
            pltpu.SemaphoreType.DMA((4,)),
        ],
        name="gram_rows",
    )(mine, other)


def exchange(pieces, axes):
    return lax.all_to_all(pieces, axes, split_axis=0, concat_axis=0, tiled=True)


def gather_sum(part, axes, count):
    return jnp.sum(exchange(jnp.broadcast_to(part, (count,) + part.shape), axes), axis=0)


def shards(y, vel):
    species, rows, depth, width = y.shape
    gy, gz, gx = ("zpair", "znear", "core"), ("x", "zhi"), ("gx",)
    inner, outer, za, zb, xs = pack(y)

    def cross(count):
        return [(i, (i + 1) % count if i % 2 else (i - 1) % count) for i in range(count)]

    up = [(i, (i + 1) % 4) for i in range(4)]
    swap = [(0, 1), (1, 0)]
    za = lax.ppermute(za, "zhi", swap)
    zb = lax.ppermute(zb, gz, cross(8))
    inner = lax.ppermute(inner, "core", swap)
    outer = lax.ppermute(outer, gy, cross(16))
    xlow = lax.ppermute(xs, gx, up)
    xhigh = lax.ppermute(xs, gx, [(target, source) for source, target in up])
    base = along_z(y, vel, za, zb)
    updated = along_xy(y, vel, base, outer, inner, xlow, xhigh)
    mine, other = gram_blocks(exchange(updated.reshape(4, species * rows * depth // 4, width), gx))
    mine = mine + lax.ppermute(other, "core", swap)
    plane = ("gx", "x")
    part = jnp.sum(exchange(mine.reshape(16, -1, 128), plane), axis=0)
    part = gather_sum(part, ("znear",), 4)
    part = gather_sum(part, ("zpair", "zhi"), 4)
    mine = exchange(jnp.broadcast_to(part, (16,) + part.shape), plane).reshape(-1, 128)
    other = lax.ppermute(mine, "core", swap)
    cells = species * rows * 16 * depth * 8
    return updated, gram_rows(mine, other, 1.0 / cells)


def solution(mesh):
    axes = ("gx", "zpair", "znear", "core", "x", "zhi")
    fine = Mesh(mesh.devices.reshape(4, 2, 4, 2, 4, 2), axes)
    grid = P(None, ("zpair", "znear", "core"), ("x", "zhi"), "gx")
    return jax.shard_map(
        shards, mesh=fine, in_specs=(grid, grid), out_specs=(grid, P("gx", None)), check_vma=False
    )
```

```python
import functools

import jax
import jax.numpy as jnp
from jax import lax
from jax.experimental import pallas as pl
from jax.experimental.pallas import tpu as pltpu
from jax.sharding import Mesh, PartitionSpec as P

C1 = (4.0 / 5.0, -1.0 / 5.0, 4.0 / 105.0, -1.0 / 280.0)
C2 = (-205.0 / 72.0, 8.0 / 5.0, -1.0 / 5.0, 8.0 / 315.0, -1.0 / 560.0)
DIFF = (0.10, 0.12, 0.08, 0.15)
NU = (-1.0, -1.0, 2.0, 0.0)
PAIRS = [(a, b) for a in range(4) for b in range(a, 4)]
MIB = 1 << 20


def split(value):
    high = value.astype(jnp.bfloat16)
    return high, (value - high.astype(jnp.float32)).astype(jnp.bfloat16)


def x_matrices(width):
    row = lax.broadcasted_iota(jnp.int32, (2 * width, width), 0)
    cell = jnp.where(row < width, row, jnp.where(row < width + 4, row - width - 4, row - 4))
    cell = jnp.where(row < width + 8, cell, 4 * width)
    step = cell - lax.broadcasted_iota(jnp.int32, (2 * width, width), 1)
    first = jnp.zeros((2 * width, width), jnp.float32)
    second = jnp.where(step == 0, jnp.float32(C2[0]), first)
    for k in range(1, 5):
        first = jnp.where(step == k, jnp.float32(C1[k - 1]), first)
        first = jnp.where(step == -k, jnp.float32(-C1[k - 1]), first)
        second = jnp.where(jnp.abs(step) == k, jnp.float32(C2[k]), second)
    return jnp.concatenate([first, second], axis=1)


def dot(left, right):
    return lax.dot_general(
        left, right, (((1,), (0,)), ((), ())), preferred_element_type=jnp.float32
    )


def lanes():
    return lax.broadcasted_iota(jnp.int32, (8, 128), 1)


def pack_body(y, inner, outer, za, zb, xs):
    count, rows, depth, width = y.shape
    core, half = lax.axis_index("core"), lax.axis_index("zhi")
    lane = lanes()

    def species(s, carry):
        inner[s] = y[s, pl.ds(4 * (1 - core), 4)]
        outer[s] = y[s, pl.ds(4 * core, 4)]
        for j in range(rows):
            low, high = y[s, j, 0:4], y[s, j, depth - 4 :]
            at = 4 * (j % 2)
            za[s, j // 2, at : at + 4] = jnp.where(half == 0, high, low)
            zb[s, j // 2, at : at + 4] = jnp.where(half == 0, low, high)
            packed = jnp.zeros((8, width), jnp.float32)
            for g in range(depth // 8):
                turned = pltpu.roll(y[s, j, 8 * g : 8 * g + 8], 8 * g + 4, 1)
                packed = jnp.where(lane // 8 == g, turned, packed)
            xs[s, j] = packed
        return carry

    lax.fori_loop(0, count, species, 0)


VMEM = pl.BlockSpec(memory_space=pltpu.VMEM)


def pack(y):
    count, rows, depth, width = y.shape
    shapes = [(count, 4, depth, width)] * 2 + [(count, rows // 2, 8, width)] * 2
    shapes = shapes + [(count, rows, 8, width)]
    return pl.pallas_call(
        pack_body,
        out_shape=[jax.ShapeDtypeStruct(shape, jnp.float32) for shape in shapes],
        in_specs=[VMEM],
        out_specs=[VMEM] * 5,
        compiler_params=pltpu.CompilerParams(vmem_limit_bytes=24 * MIB),
        name="pack",
    )(y)


def factors(s, count):
    diff = jnp.float32(0.25 * DIFF[0])
    nu = jnp.float32(NU[0])
    for q in range(1, count):
        diff = jnp.where(s == q, jnp.float32(0.25 * DIFF[q]), diff)
        nu = jnp.where(s == q, jnp.float32(NU[q]), nu)
    return diff, nu


def along_z_body(y, vel, base, za, zb, out, rate, pad):
    count, rows, depth, width = y.shape
    half = lax.axis_index("zhi")
    for j in range(rows):
        heat = 1.0 + 3.0 * y[2, j]
        rate[j] = y[0, j] * y[1, j] * jnp.exp(-3.0 / heat)

    def species(s, carry):
        diff, nu = factors(s, count)
        for j in range(rows):
            at = 4 * (j % 2)
            fa, fb = za[s, j // 2, at : at + 4], zb[s, j // 2, at : at + 4]
            pad[j, 4:8] = jnp.where(half == 0, fb, fa)
            pad[j, 8 : 8 + depth] = y[s, j]
            pad[j, 8 + depth : 12 + depth] = jnp.where(half == 0, fa, fb)
        for j in range(rows):
            centre = y[s, j]
            first = None
            second = (2.0 * C2[0]) * centre
            for k in range(1, 5):
                ahead, behind = pad[j, 8 + k : 8 + k + depth], pad[j, 8 - k : 8 - k + depth]
                term = (0.25 * C1[k - 1]) * (ahead - behind)
                first = term if first is None else first + term
                second = second + C2[k] * (ahead + behind)
            out[s, j] = (centre + base[s, j]) + (diff * second - vel[2, j] * first + nu * rate[j])
        return carry

    lax.fori_loop(0, count, species, 0)


def along_z(y, *rest):
    _, rows, depth, width = y.shape
    return pl.pallas_call(
        along_z_body,
        out_shape=jax.ShapeDtypeStruct(y.shape, jnp.float32),
        in_specs=[VMEM] * (1 + len(rest)),
        out_specs=VMEM,
        scratch_shapes=[
            pltpu.VMEM((rows, depth, width), jnp.float32),
            pltpu.VMEM((rows, depth + 16, width), jnp.float32),
        ],
        compiler_params=pltpu.CompilerParams(vmem_limit_bytes=24 * MIB),
        name="along_z",
    )(y, *rest)


def along_xy_body(y, vel, outer, inner, xlow, xhigh, out, side, dx, pad):
    count, rows, depth, width = y.shape
    core = lax.axis_index("core")
    below = lanes() % 8 < 4
    mh, ml = split(x_matrices(width))

    def species(s, carry):
        diff, _ = factors(s, count)
        pad[pl.ds(12 * (1 - core), 4)] = inner[s]
        pad[pl.ds(12 * core, 4)] = outer[s]
        pad[4 : 4 + rows] = y[s]
        for j in range(rows):
            packed = jnp.where(below, xlow[s, j], xhigh[s, j])
            for g in range(depth // 8):
                row = j * depth + 8 * g
                side[row : row + 8] = pltpu.roll(packed, (128 - 8 * g) % 128, 1)
        left = jnp.concatenate([y[s].reshape(rows * depth, width), side[...]], axis=1)
        high, low = split(left)
        dx[...] = dot(high, mh) + (dot(low, mh) + dot(high, ml))
        for j in range(rows):
            first = None
            second = dx[j * depth : (j + 1) * depth, width:]
            for k in range(1, 5):
                ahead, behind = pad[4 + j + k], pad[4 + j - k]
                term = (0.25 * C1[k - 1]) * (ahead - behind)
                first = term if first is None else first + term
                second = second + C2[k] * (ahead + behind)
            moved = (0.25 * vel[0, j]) * dx[j * depth : (j + 1) * depth, :width]
            out[s, j] = diff * second - (moved + vel[1, j] * first)
        return carry

    lax.fori_loop(0, count, species, 0)


def along_xy(y, *rest):
    _, rows, depth, width = y.shape
    return pl.pallas_call(
        along_xy_body,
        out_shape=jax.ShapeDtypeStruct(y.shape, jnp.float32),
        in_specs=[VMEM] * (1 + len(rest)),
        out_specs=VMEM,
        scratch_shapes=[
            pltpu.VMEM((rows * depth, width), jnp.float32),
            pltpu.VMEM((rows * depth, 2 * width), jnp.float32),
            pltpu.VMEM((rows + 8, depth, width), jnp.float32),
        ],
        compiler_params=pltpu.CompilerParams(vmem_limit_bytes=32 * MIB),
        cost_estimate=pl.CostEstimate(
            flops=10**9, bytes_accessed=10**7, transcendentals=0
        ),
        name="along_xy",
    )(y, *rest)


def products(lines):
    whole = jnp.concatenate([lines[a] for a in range(lines.shape[0])], axis=1)
    high, low = split(whole)
    turned_high, turned_low = split(whole.T)
    total = dot(turned_high, high) + (dot(turned_high, low) + dot(turned_low, high))
    return [total[a * 128 : (a + 1) * 128, b * 128 : (b + 1) * 128] for a, b in PAIRS]


def gram_body(lines, mine, other):
    core = lax.axis_index("core")
    tiles = products(lines)
    for q in range(5):
        at = slice(q * 128, (q + 1) * 128)
        mine[at] = jnp.where(core == 0, tiles[q], tiles[q + 5])
        other[at] = jnp.where(core == 0, tiles[q + 5], tiles[q])


def gram_blocks(lines):
    return pl.pallas_call(
        gram_body,
        out_shape=[jax.ShapeDtypeStruct((len(PAIRS) * 64, 128), jnp.float32)] * 2,
        in_specs=[VMEM],
        out_specs=[VMEM] * 2,
        compiler_params=pltpu.CompilerParams(vmem_limit_bytes=40 * MIB),
        name="gram",
    )(lines)


def rows_body(scale, mine, other, out, tiles, sems):
    row, core = lax.axis_index("gx"), lax.axis_index("core")

    def tile(b):
        low, top = jnp.minimum(row, b), jnp.maximum(row, b)
        index = low * 4 - (low * (low - 1)) // 2 + (top - low)
        owner = jnp.where(index >= 5, 1, 0)
        at = pl.ds(pl.multiple_of((index - 5 * owner) * 128, 128), 128)
        return owner == core, at

    for b in range(4):
        here, at = tile(b)

        @pl.when(here)
        def _():
            pltpu.make_async_copy(mine.at[at], tiles.at[b], sems.at[b]).start()

        @pl.when(jnp.logical_not(here))
        def _():
            pltpu.make_async_copy(other.at[at], tiles.at[b], sems.at[b]).start()

    for b in range(4):
        pltpu.make_async_copy(mine.at[pl.ds(0, 128)], tiles.at[b], sems.at[b]).wait()
        block = tiles[b] * scale
        out[:, b * 128 : (b + 1) * 128] = jnp.where(row <= b, block, block.T)


def gram_rows(mine, other, scale):
    return pl.pallas_call(
        functools.partial(rows_body, scale),
        out_shape=jax.ShapeDtypeStruct((128, 512), jnp.float32),
        in_specs=[pl.BlockSpec(memory_space=pl.ANY)] * 2,
        out_specs=VMEM,
        scratch_shapes=[
            pltpu.VMEM((4, 128, 128), jnp.float32),
            pltpu.SemaphoreType.DMA((4,)),
        ],
        name="gram_rows",
    )(mine, other)


def exchange(pieces, axes):
    return lax.all_to_all(pieces, axes, split_axis=0, concat_axis=0, tiled=True)


def gather_sum(part, axes, count):
    return jnp.sum(exchange(jnp.broadcast_to(part, (count,) + part.shape), axes), axis=0)


def shards(y, vel):
    species, rows, depth, width = y.shape
    gy, gz, gx = ("zpair", "znear", "core"), ("x", "zhi"), ("gx",)
    inner, outer, za, zb, xs = pack(y)

    def cross(count):
        return [(i, (i + 1) % count if i % 2 else (i - 1) % count) for i in range(count)]

    up = [(i, (i + 1) % 4) for i in range(4)]
    swap = [(0, 1), (1, 0)]
    za = lax.ppermute(za, "zhi", swap)
    zb = lax.ppermute(zb, gz, cross(8))
    inner = lax.ppermute(inner, "core", swap)
    outer = lax.ppermute(outer, gy, cross(16))
    xlow = lax.ppermute(xs, gx, up)
    xhigh = lax.ppermute(xs, gx, [(target, source) for source, target in up])
    base = along_xy(y, vel, outer, inner, xlow, xhigh)
    updated = along_z(y, vel, base, za, zb)
    mine, other = gram_blocks(exchange(updated.reshape(4, species * rows * depth // 4, width), gx))
    mine = mine + lax.ppermute(other, "core", swap)
    plane = ("gx", "x")
    part = jnp.sum(exchange(mine.reshape(16, -1, 128), plane), axis=0)
    part = gather_sum(part, ("znear",), 4)
    part = gather_sum(part, ("zpair", "zhi"), 4)
    mine = exchange(jnp.broadcast_to(part, (16,) + part.shape), plane).reshape(-1, 128)
    other = lax.ppermute(mine, "core", swap)
    cells = species * rows * 16 * depth * 8
    return updated, gram_rows(mine, other, 1.0 / cells)


def solution(mesh):
    axes = ("gx", "zpair", "znear", "core", "x", "zhi")
    fine = Mesh(mesh.devices.reshape(4, 2, 4, 2, 4, 2), axes)
    grid = P(None, ("zpair", "znear", "core"), ("x", "zhi"), "gx")
    return jax.shard_map(
        shards, mesh=fine, in_specs=(grid, grid), out_specs=(grid, P("gx", None)), check_vma=False
    )
```

```python
import functools

import jax
import jax.numpy as jnp
from jax import lax
from jax.experimental import pallas as pl
from jax.experimental.pallas import tpu as pltpu
from jax.sharding import Mesh, PartitionSpec as P

C1 = (4.0 / 5.0, -1.0 / 5.0, 4.0 / 105.0, -1.0 / 280.0)
C2 = (-205.0 / 72.0, 8.0 / 5.0, -1.0 / 5.0, 8.0 / 315.0, -1.0 / 560.0)
DIFF = (0.10, 0.12, 0.08, 0.15)
NU = (-1.0, -1.0, 2.0, 0.0)
PAIRS = [(a, b) for a in range(4) for b in range(a, 4)]
MIB = 1 << 20


def split(value):
    high = value.astype(jnp.bfloat16)
    return high, (value - high.astype(jnp.float32)).astype(jnp.bfloat16)


def x_matrices(width):
    row = lax.broadcasted_iota(jnp.int32, (2 * width, width), 0)
    cell = jnp.where(row < width, row, jnp.where(row < width + 4, row - width - 4, row - 4))
    cell = jnp.where(row < width + 8, cell, 4 * width)
    step = cell - lax.broadcasted_iota(jnp.int32, (2 * width, width), 1)
    first = jnp.zeros((2 * width, width), jnp.float32)
    second = jnp.where(step == 0, jnp.float32(C2[0]), first)
    for k in range(1, 5):
        first = jnp.where(step == k, jnp.float32(C1[k - 1]), first)
        first = jnp.where(step == -k, jnp.float32(-C1[k - 1]), first)
        second = jnp.where(jnp.abs(step) == k, jnp.float32(C2[k]), second)
    return jnp.concatenate([first, second], axis=1)


def dot(left, right):
    return lax.dot_general(
        left, right, (((1,), (0,)), ((), ())), preferred_element_type=jnp.float32
    )


def lanes():
    return lax.broadcasted_iota(jnp.int32, (8, 128), 1)


def pack_body(y, inner, outer, keep, xs):
    count, rows, depth, width = y.shape
    core, half = lax.axis_index("core"), lax.axis_index("zhi")
    lane = lanes()

    def species(s, carry):
        swap = 4 * depth
        inner[s, 0:swap] = y[s, pl.ds(4 * (1 - core), 4)].reshape(swap, width)
        outer[s] = y[s, pl.ds(4 * core, 4)]
        for j in range(rows):
            low, high = y[s, j, 0:4], y[s, j, depth - 4 :]
            at = 4 * j
            keep[s, at : at + 4] = jnp.where(half == core, high, low)
            inner[s, swap + at : swap + at + 4] = jnp.where(half == core, low, high)
            packed = jnp.zeros((8, width), jnp.float32)
            for g in range(depth // 8):
                turned = pltpu.roll(y[s, j, 8 * g : 8 * g + 8], 8 * g + 4, 1)
                packed = jnp.where(lane // 8 == g, turned, packed)
            xs[s, j] = packed
        return carry

    lax.fori_loop(0, count, species, 0)


VMEM = pl.BlockSpec(memory_space=pltpu.VMEM)


def pack(y):
    count, rows, depth, width = y.shape
    shapes = [(count, 4 * depth + 4 * rows, width), (count, 4, depth, width)]
    shapes = shapes + [(count, 4 * rows, width), (count, rows, 8, width)]
    return pl.pallas_call(
        pack_body,
        out_shape=[jax.ShapeDtypeStruct(shape, jnp.float32) for shape in shapes],
        in_specs=[VMEM],
        out_specs=[VMEM] * 4,
        compiler_params=pltpu.CompilerParams(vmem_limit_bytes=24 * MIB),
        name="pack",
    )(y)


def factors(s, count):
    diff = jnp.float32(0.25 * DIFF[0])
    nu = jnp.float32(NU[0])
    for q in range(1, count):
        diff = jnp.where(s == q, jnp.float32(0.25 * DIFF[q]), diff)
        nu = jnp.where(s == q, jnp.float32(NU[q]), nu)
    return diff, nu


def along_z_body(y, vel, base, direct, carried, out, rate, pad):
    count, rows, depth, width = y.shape
    apart = lax.axis_index("zhi") != lax.axis_index("core")
    for j in range(rows):
        heat = 1.0 + 3.0 * y[2, j]
        rate[j] = y[0, j] * y[1, j] * jnp.exp(-3.0 / heat)

    def species(s, carry):
        diff, nu = factors(s, count)
        for j in range(rows):
            at = 4 * j
            fa, fb = direct[0, s, at : at + 4], carried[s, at : at + 4]
            pad[j, 4:8] = jnp.where(apart, fa, fb)
            pad[j, 8 : 8 + depth] = y[s, j]
            pad[j, 8 + depth : 12 + depth] = jnp.where(apart, fb, fa)
        for j in range(rows):
            centre = y[s, j]
            first = None
            second = (2.0 * C2[0]) * centre
            for k in range(1, 5):
                ahead, behind = pad[j, 8 + k : 8 + k + depth], pad[j, 8 - k : 8 - k + depth]
                term = (0.25 * C1[k - 1]) * (ahead - behind)
                first = term if first is None else first + term
                second = second + C2[k] * (ahead + behind)
            out[s, j] = (centre + base[s, j]) + (diff * second - vel[2, j] * first + nu * rate[j])
        return carry

    lax.fori_loop(0, count, species, 0)


def along_z(y, *rest):
    _, rows, depth, width = y.shape
    return pl.pallas_call(
        along_z_body,
        out_shape=jax.ShapeDtypeStruct(y.shape, jnp.float32),
        in_specs=[VMEM] * (1 + len(rest)),
        out_specs=VMEM,
        scratch_shapes=[
            pltpu.VMEM((rows, depth, width), jnp.float32),
            pltpu.VMEM((rows, depth + 16, width), jnp.float32),
        ],
        compiler_params=pltpu.CompilerParams(vmem_limit_bytes=24 * MIB),
        name="along_z",
    )(y, *rest)


def along_xy_body(y, vel, outer, inner, xlow, xhigh, out, side, dx, pad):
    count, rows, depth, width = y.shape
    core = lax.axis_index("core")
    below = lanes() % 8 < 4
    mh, ml = split(x_matrices(width))

    def species(s, carry):
        diff, _ = factors(s, count)
        pad[pl.ds(12 * (1 - core), 4)] = inner[s, 0 : 4 * depth].reshape(4, depth, width)
        pad[pl.ds(12 * core, 4)] = outer[s]
        pad[4 : 4 + rows] = y[s]
        for j in range(rows):
            packed = jnp.where(below, xlow[s, j], xhigh[s, j])
            for g in range(depth // 8):
                row = j * depth + 8 * g
                side[row : row + 8] = pltpu.roll(packed, (128 - 8 * g) % 128, 1)
        left = jnp.concatenate([y[s].reshape(rows * depth, width), side[...]], axis=1)
        high, low = split(left)
        dx[...] = dot(high, mh) + (dot(low, mh) + dot(high, ml))
        for j in range(rows):
            first = None
            second = dx[j * depth : (j + 1) * depth, width:]
            for k in range(1, 5):
                ahead, behind = pad[4 + j + k], pad[4 + j - k]
                term = (0.25 * C1[k - 1]) * (ahead - behind)
                first = term if first is None else first + term
                second = second + C2[k] * (ahead + behind)
            moved = (0.25 * vel[0, j]) * dx[j * depth : (j + 1) * depth, :width]
            out[s, j] = diff * second - (moved + vel[1, j] * first)
        return carry

    lax.fori_loop(0, count, species, 0)


def along_xy(y, *rest):
    _, rows, depth, width = y.shape
    return pl.pallas_call(
        along_xy_body,
        out_shape=jax.ShapeDtypeStruct(y.shape, jnp.float32),
        in_specs=[VMEM] * (1 + len(rest)),
        out_specs=VMEM,
        scratch_shapes=[
            pltpu.VMEM((rows * depth, width), jnp.float32),
            pltpu.VMEM((rows * depth, 2 * width), jnp.float32),
            pltpu.VMEM((rows + 8, depth, width), jnp.float32),
        ],
        compiler_params=pltpu.CompilerParams(vmem_limit_bytes=32 * MIB),
        cost_estimate=pl.CostEstimate(
            flops=10**9, bytes_accessed=10**7, transcendentals=0
        ),
        name="along_xy",
    )(y, *rest)


def products(lines):
    whole = jnp.concatenate([lines[a] for a in range(lines.shape[0])], axis=1)
    high, low = split(whole)
    turned_high, turned_low = split(whole.T)
    total = dot(turned_high, high) + (dot(turned_high, low) + dot(turned_low, high))
    return [total[a * 128 : (a + 1) * 128, b * 128 : (b + 1) * 128] for a, b in PAIRS]


def gram_body(lines, mine, other):
    core = lax.axis_index("core")
    tiles = products(lines)
    for q in range(5):
        at = slice(q * 128, (q + 1) * 128)
        mine[at] = jnp.where(core == 0, tiles[q], tiles[q + 5])
        other[at] = jnp.where(core == 0, tiles[q + 5], tiles[q])


def gram_blocks(lines):
    return pl.pallas_call(
        gram_body,
        out_shape=[jax.ShapeDtypeStruct((len(PAIRS) * 64, 128), jnp.float32)] * 2,
        in_specs=[VMEM],
        out_specs=[VMEM] * 2,
        compiler_params=pltpu.CompilerParams(vmem_limit_bytes=40 * MIB),
        name="gram",
    )(lines)


def rows_body(scale, mine, other, out, tiles, sems):
    row, core = lax.axis_index("gx"), lax.axis_index("core")

    def tile(b):
        low, top = jnp.minimum(row, b), jnp.maximum(row, b)
        index = low * 4 - (low * (low - 1)) // 2 + (top - low)
        owner = jnp.where(index >= 5, 1, 0)
        at = pl.ds(pl.multiple_of((index - 5 * owner) * 128, 128), 128)
        return owner == core, at

    for b in range(4):
        here, at = tile(b)

        @pl.when(here)
        def _():
            pltpu.make_async_copy(mine.at[at], tiles.at[b], sems.at[b]).start()

        @pl.when(jnp.logical_not(here))
        def _():
            pltpu.make_async_copy(other.at[at], tiles.at[b], sems.at[b]).start()

    for b in range(4):
        pltpu.make_async_copy(mine.at[pl.ds(0, 128)], tiles.at[b], sems.at[b]).wait()
        block = tiles[b] * scale
        out[:, b * 128 : (b + 1) * 128] = jnp.where(row <= b, block, block.T)


def gram_rows(mine, other, scale):
    return pl.pallas_call(
        functools.partial(rows_body, scale),
        out_shape=jax.ShapeDtypeStruct((128, 512), jnp.float32),
        in_specs=[pl.BlockSpec(memory_space=pl.ANY)] * 2,
        out_specs=VMEM,
        scratch_shapes=[
            pltpu.VMEM((4, 128, 128), jnp.float32),
            pltpu.SemaphoreType.DMA((4,)),
        ],
        name="gram_rows",
    )(mine, other)


def exchange(pieces, axes):
    return lax.all_to_all(pieces, axes, split_axis=0, concat_axis=0, tiled=True)


def gather_sum(part, axes, count):
    return jnp.sum(exchange(jnp.broadcast_to(part, (count,) + part.shape), axes), axis=0)


def shards(y, vel):
    species, rows, depth, width = y.shape
    gy, gz, gx = ("zpair", "znear", "core"), ("x", "zhi"), ("gx",)
    inner, outer, keep, xs = pack(y)

    def cross(count):
        return [(i, (i + 1) % count if i % 2 else (i - 1) % count) for i in range(count)]

    up = [(i, (i + 1) % 4) for i in range(4)]
    swap = [(0, 1), (1, 0)]
    outer = lax.ppermute(outer, gy, cross(16))
    inner = lax.ppermute(inner, "core", swap)
    xlow = lax.ppermute(xs, gx, up)
    xhigh = lax.ppermute(xs, gx, [(target, source) for source, target in up])
    pairs = [(i, i ^ 1) for i in range(8)] + [(8 + i, 8 + j) for i, j in cross(8)]
    faces = jnp.stack([keep, inner[:, 4 * depth :]])
    faces = lax.ppermute(faces, ("core",) + gz, pairs)
    carried = lax.ppermute(faces[1], "core", swap)
    base = along_xy(y, vel, outer, inner, xlow, xhigh)
    updated = along_z(y, vel, base, faces, carried)
    mine, other = gram_blocks(exchange(updated.reshape(4, species * rows * depth // 4, width), gx))
    mine = mine + lax.ppermute(other, "core", swap)
    plane = ("gx", "x")
    part = jnp.sum(exchange(mine.reshape(16, -1, 128), plane), axis=0)
    part = gather_sum(part, ("znear",), 4)
    part = gather_sum(part, ("zpair", "zhi"), 4)
    mine = exchange(jnp.broadcast_to(part, (16,) + part.shape), plane).reshape(-1, 128)
    other = lax.ppermute(mine, "core", swap)
    cells = species * rows * 16 * depth * 8
    return updated, gram_rows(mine, other, 1.0 / cells)


def solution(mesh):
    axes = ("gx", "zpair", "znear", "core", "x", "zhi")
    fine = Mesh(mesh.devices.reshape(4, 2, 4, 2, 4, 2), axes)
    grid = P(None, ("zpair", "znear", "core"), ("x", "zhi"), "gx")
    return jax.shard_map(
        shards, mesh=fine, in_specs=(grid, grid), out_specs=(grid, P("gx", None)), check_vma=False
    )
```

```python
import functools

import jax
import jax.numpy as jnp
from jax import lax
from jax.experimental import pallas as pl
from jax.experimental.pallas import tpu as pltpu
from jax.sharding import Mesh, PartitionSpec as P

C1 = (4.0 / 5.0, -1.0 / 5.0, 4.0 / 105.0, -1.0 / 280.0)
C2 = (-205.0 / 72.0, 8.0 / 5.0, -1.0 / 5.0, 8.0 / 315.0, -1.0 / 560.0)
DIFF = (0.10, 0.12, 0.08, 0.15)
NU = (-1.0, -1.0, 2.0, 0.0)
PAIRS = [(a, b) for a in range(4) for b in range(a, 4)]
MIB = 1 << 20


def split(value):
    high = value.astype(jnp.bfloat16)
    return high, (value - high.astype(jnp.float32)).astype(jnp.bfloat16)


def x_matrices(width):
    row = lax.broadcasted_iota(jnp.int32, (2 * width, width), 0)
    cell = jnp.where(row < width, row, jnp.where(row < width + 4, row - width - 4, row - 4))
    cell = jnp.where(row < width + 8, cell, 4 * width)
    step = cell - lax.broadcasted_iota(jnp.int32, (2 * width, width), 1)
    first = jnp.zeros((2 * width, width), jnp.float32)
    second = jnp.where(step == 0, jnp.float32(C2[0]), first)
    for k in range(1, 5):
        first = jnp.where(step == k, jnp.float32(C1[k - 1]), first)
        first = jnp.where(step == -k, jnp.float32(-C1[k - 1]), first)
        second = jnp.where(jnp.abs(step) == k, jnp.float32(C2[k]), second)
    return jnp.concatenate([first, second], axis=1)


def dot(left, right):
    return lax.dot_general(
        left, right, (((1,), (0,)), ((), ())), preferred_element_type=jnp.float32
    )


def lanes():
    return lax.broadcasted_iota(jnp.int32, (8, 128), 1)


def pack_body(y, inner, outer, za, zb, xs):
    count, rows, depth, width = y.shape
    core, half = lax.axis_index("core"), lax.axis_index("zhi")
    lane = lanes()

    def species(s, carry):
        inner[s] = y[s, pl.ds(4 * (1 - core), 4)]
        outer[s] = y[s, pl.ds(4 * core, 4)]
        for j in range(rows):
            low, high = y[s, j, 0:4], y[s, j, depth - 4 :]
            at = 4 * (j % 2)
            za[s, j // 2, at : at + 4] = jnp.where(half == 0, high, low)
            zb[s, j // 2, at : at + 4] = jnp.where(half == 0, low, high)
            packed = jnp.zeros((8, width), jnp.float32)
            for g in range(depth // 8):
                turned = pltpu.roll(y[s, j, 8 * g : 8 * g + 8], 8 * g + 4, 1)
                packed = jnp.where(lane // 8 == g, turned, packed)
            xs[s, j] = packed
        return carry

    lax.fori_loop(0, count, species, 0)


VMEM = pl.BlockSpec(memory_space=pltpu.VMEM)


def pack(y):
    count, rows, depth, width = y.shape
    shapes = [(count, 4, depth, width)] * 2 + [(count, rows // 2, 8, width)] * 2
    shapes = shapes + [(count, rows, 8, width)]
    return pl.pallas_call(
        pack_body,
        out_shape=[jax.ShapeDtypeStruct(shape, jnp.float32) for shape in shapes],
        in_specs=[VMEM],
        out_specs=[VMEM] * 5,
        compiler_params=pltpu.CompilerParams(vmem_limit_bytes=14 * MIB),
        name="pack",
    )(y)


def factors(s, count):
    diff = jnp.float32(0.25 * DIFF[0])
    nu = jnp.float32(NU[0])
    for q in range(1, count):
        diff = jnp.where(s == q, jnp.float32(0.25 * DIFF[q]), diff)
        nu = jnp.where(s == q, jnp.float32(NU[q]), nu)
    return diff, nu


def along_z_body(y, vel, za, zb, out, rate, pad):
    count, rows, depth, width = y.shape
    half = lax.axis_index("zhi")
    for j in range(rows):
        heat = 1.0 + 3.0 * y[2, j]
        rate[j] = y[0, j] * y[1, j] * jnp.exp(-3.0 / heat)

    def species(s, carry):
        diff, nu = factors(s, count)
        for j in range(rows):
            at = 4 * (j % 2)
            fa, fb = za[s, j // 2, at : at + 4], zb[s, j // 2, at : at + 4]
            pad[j, 4:8] = jnp.where(half == 0, fb, fa)
            pad[j, 8 : 8 + depth] = y[s, j]
            pad[j, 8 + depth : 12 + depth] = jnp.where(half == 0, fa, fb)
        for j in range(rows):
            centre = y[s, j]
            first = None
            second = (2.0 * C2[0]) * centre
            for k in range(1, 5):
                ahead, behind = pad[j, 8 + k : 8 + k + depth], pad[j, 8 - k : 8 - k + depth]
                term = (0.25 * C1[k - 1]) * (ahead - behind)
                first = term if first is None else first + term
                second = second + C2[k] * (ahead + behind)
            out[s, j] = centre + (diff * second - vel[2, j] * first + nu * rate[j])
        return carry

    lax.fori_loop(0, count, species, 0)


def along_z(y, *rest):
    _, rows, depth, width = y.shape
    return pl.pallas_call(
        along_z_body,
        out_shape=jax.ShapeDtypeStruct(y.shape, jnp.float32),
        in_specs=[VMEM] * (1 + len(rest)),
        out_specs=VMEM,
        scratch_shapes=[
            pltpu.VMEM((rows, depth, width), jnp.float32),
            pltpu.VMEM((rows, depth + 16, width), jnp.float32),
        ],
        compiler_params=pltpu.CompilerParams(vmem_limit_bytes=14 * MIB),
        cost_estimate=pl.CostEstimate(
            flops=10**9, bytes_accessed=10**7, transcendentals=0
        ),
        name="along_z",
    )(y, *rest)


def along_xy_body(y, vel, base, outer, inner, xlow, xhigh, result, side, dx, pad, out, sems):
    count, rows, depth, width = y.shape
    core = lax.axis_index("core")
    below = lanes() % 8 < 4
    mh, ml = split(x_matrices(width))

    def species(s, carry):
        diff, _ = factors(s, count)
        pad[pl.ds(12 * (1 - core), 4)] = inner[s]
        pad[pl.ds(12 * core, 4)] = outer[s]
        pad[4 : 4 + rows] = y[s]
        for j in range(rows):
            packed = jnp.where(below, xlow[s, j], xhigh[s, j])
            for g in range(depth // 8):
                row = j * depth + 8 * g
                side[row : row + 8] = pltpu.roll(packed, (128 - 8 * g) % 128, 1)
        left = jnp.concatenate([y[s].reshape(rows * depth, width), side[...]], axis=1)
        high, low = split(left)
        dx[...] = dot(high, mh) + (dot(low, mh) + dot(high, ml))
        for j in range(rows):
            first = None
            second = dx[j * depth : (j + 1) * depth, width:]
            for k in range(1, 5):
                ahead, behind = pad[4 + j + k], pad[4 + j - k]
                term = (0.25 * C1[k - 1]) * (ahead - behind)
                first = term if first is None else first + term
                second = second + C2[k] * (ahead + behind)
            moved = (0.25 * vel[0, j]) * dx[j * depth : (j + 1) * depth, :width]
            out[s, j] = base[s, j] + (diff * second - (moved + vel[1, j] * first))
        pltpu.make_async_copy(out.at[s], result.at[s], sems.at[s]).start()
        return carry

    lax.fori_loop(0, count, species, 0)
    for s in range(count):
        pltpu.make_async_copy(out.at[s], result.at[s], sems.at[s]).wait()


def along_xy(y, *rest):
    _, rows, depth, width = y.shape
    return pl.pallas_call(
        along_xy_body,
        out_shape=jax.ShapeDtypeStruct(y.shape, jnp.float32),
        in_specs=[VMEM] * (1 + len(rest)),
        out_specs=pl.BlockSpec(memory_space=pl.ANY),
        scratch_shapes=[
            pltpu.VMEM((rows * depth, width), jnp.float32),
            pltpu.VMEM((rows * depth, 2 * width), jnp.float32),
            pltpu.VMEM((rows + 8, depth, width), jnp.float32),
            pltpu.VMEM(y.shape, jnp.float32),
            pltpu.SemaphoreType.DMA((y.shape[0],)),
        ],
        compiler_params=pltpu.CompilerParams(vmem_limit_bytes=16 * MIB),
        name="along_xy",
    )(y, *rest)


def products(lines):
    whole = jnp.concatenate([lines[a] for a in range(lines.shape[0])], axis=1)
    high, low = split(whole)
    turned_high, turned_low = split(whole.T)
    total = dot(turned_high, high) + (dot(turned_high, low) + dot(turned_low, high))
    return [total[a * 128 : (a + 1) * 128, b * 128 : (b + 1) * 128] for a, b in PAIRS]


def gram_body(lines, mine, other):
    core = lax.axis_index("core")
    tiles = products(lines)
    for q in range(5):
        at = slice(q * 128, (q + 1) * 128)
        mine[at] = jnp.where(core == 0, tiles[q], tiles[q + 5])
        other[at] = jnp.where(core == 0, tiles[q + 5], tiles[q])


def gram_blocks(lines):
    return pl.pallas_call(
        gram_body,
        out_shape=[jax.ShapeDtypeStruct((len(PAIRS) * 64, 128), jnp.float32)] * 2,
        in_specs=[VMEM],
        out_specs=[VMEM] * 2,
        compiler_params=pltpu.CompilerParams(vmem_limit_bytes=16 * MIB),
        name="gram",
    )(lines)


def rows_body(scale, mine, other, out, tiles, sems):
    row, core = lax.axis_index("gx"), lax.axis_index("core")

    def tile(b):
        low, top = jnp.minimum(row, b), jnp.maximum(row, b)
        index = low * 4 - (low * (low - 1)) // 2 + (top - low)
        owner = jnp.where(index >= 5, 1, 0)
        at = pl.ds(pl.multiple_of((index - 5 * owner) * 128, 128), 128)
        return owner == core, at

    for b in range(4):
        here, at = tile(b)

        @pl.when(here)
        def _():
            pltpu.make_async_copy(mine.at[at], tiles.at[b], sems.at[b]).start()

        @pl.when(jnp.logical_not(here))
        def _():
            pltpu.make_async_copy(other.at[at], tiles.at[b], sems.at[b]).start()

    for b in range(4):
        pltpu.make_async_copy(mine.at[pl.ds(0, 128)], tiles.at[b], sems.at[b]).wait()
        block = tiles[b] * scale
        out[:, b * 128 : (b + 1) * 128] = jnp.where(row <= b, block, block.T)


def gram_rows(mine, other, scale):
    return pl.pallas_call(
        functools.partial(rows_body, scale),
        out_shape=jax.ShapeDtypeStruct((128, 512), jnp.float32),
        in_specs=[pl.BlockSpec(memory_space=pl.ANY)] * 2,
        out_specs=VMEM,
        scratch_shapes=[
            pltpu.VMEM((4, 128, 128), jnp.float32),
            pltpu.SemaphoreType.DMA((4,)),
        ],
        compiler_params=pltpu.CompilerParams(vmem_limit_bytes=8 * MIB),
        name="gram_rows",
    )(mine, other)


def exchange(pieces, axes):
    return lax.all_to_all(pieces, axes, split_axis=0, concat_axis=0, tiled=True)


def gather_sum(part, axes, count):
    return jnp.sum(exchange(jnp.broadcast_to(part, (count,) + part.shape), axes), axis=0)


def shards(y, vel):
    species, rows, depth, width = y.shape
    gy, gz, gx = ("zpair", "znear", "core"), ("x", "zhi"), ("gx",)
    inner, outer, za, zb, xs = pack(y)

    def cross(count):
        return [(i, (i + 1) % count if i % 2 else (i - 1) % count) for i in range(count)]

    up = [(i, (i + 1) % 4) for i in range(4)]
    swap = [(0, 1), (1, 0)]
    za = lax.ppermute(za, "zhi", swap)
    zb = lax.ppermute(zb, gz, cross(8))
    inner = lax.ppermute(inner, "core", swap)
    outer = lax.ppermute(outer, gy, cross(16))
    xlow = lax.ppermute(xs, gx, up)
    xhigh = lax.ppermute(xs, gx, [(target, source) for source, target in up])
    base = along_z(y, vel, za, zb)
    updated = along_xy(y, vel, base, outer, inner, xlow, xhigh)
    mine, other = gram_blocks(exchange(updated.reshape(4, species * rows * depth // 4, width), gx))
    mine = mine + lax.ppermute(other, "core", swap)
    plane = ("gx", "x")
    part = jnp.sum(exchange(mine.reshape(16, -1, 128), plane), axis=0)
    part = gather_sum(part, ("znear",), 4)
    part = gather_sum(part, ("zpair", "zhi"), 4)
    mine = exchange(jnp.broadcast_to(part, (16,) + part.shape), plane).reshape(-1, 128)
    other = lax.ppermute(mine, "core", swap)
    cells = species * rows * 16 * depth * 8
    return updated, gram_rows(mine, other, 1.0 / cells)


def solution(mesh):
    axes = ("gx", "zpair", "znear", "core", "x", "zhi")
    fine = Mesh(mesh.devices.reshape(4, 2, 4, 2, 4, 2), axes)
    grid = P(None, ("zpair", "znear", "core"), ("x", "zhi"), "gx")
    return jax.shard_map(
        shards, mesh=fine, in_specs=(grid, grid), out_specs=(grid, P("gx", None)), check_vma=False
    )
```

```python
import functools

import jax
import jax.numpy as jnp
from jax import lax
from jax.experimental import pallas as pl
from jax.experimental.pallas import tpu as pltpu
from jax.sharding import Mesh, PartitionSpec as P

C1 = (4.0 / 5.0, -1.0 / 5.0, 4.0 / 105.0, -1.0 / 280.0)
C2 = (-205.0 / 72.0, 8.0 / 5.0, -1.0 / 5.0, 8.0 / 315.0, -1.0 / 560.0)
DIFF = (0.10, 0.12, 0.08, 0.15)
NU = (-1.0, -1.0, 2.0, 0.0)
PAIRS = [(a, b) for a in range(4) for b in range(a, 4)]
MIB = 1 << 20


def split(value):
    high = value.astype(jnp.bfloat16)
    return high, (value - high.astype(jnp.float32)).astype(jnp.bfloat16)


def x_matrices(width):
    row = lax.broadcasted_iota(jnp.int32, (2 * width, width), 0)
    cell = jnp.where(row < width, row, jnp.where(row < width + 4, row - width - 4, row - 4))
    cell = jnp.where(row < width + 8, cell, 4 * width)
    step = cell - lax.broadcasted_iota(jnp.int32, (2 * width, width), 1)
    first = jnp.zeros((2 * width, width), jnp.float32)
    second = jnp.where(step == 0, jnp.float32(C2[0]), first)
    for k in range(1, 5):
        first = jnp.where(step == k, jnp.float32(C1[k - 1]), first)
        first = jnp.where(step == -k, jnp.float32(-C1[k - 1]), first)
        second = jnp.where(jnp.abs(step) == k, jnp.float32(C2[k]), second)
    return jnp.concatenate([first, second], axis=1)


def dot(left, right):
    return lax.dot_general(
        left, right, (((1,), (0,)), ((), ())), preferred_element_type=jnp.float32
    )


def lanes():
    return lax.broadcasted_iota(jnp.int32, (8, 128), 1)


def pack_body(y, inner, outer, za, zb, xs):
    count, rows, depth, width = y.shape
    core, half = lax.axis_index("core"), lax.axis_index("zhi")
    lane = lanes()

    def species(s, carry):
        inner[s] = y[s, pl.ds(4 * (1 - core), 4)]
        outer[s] = y[s, pl.ds(4 * core, 4)]
        for j in range(rows):
            low, high = y[s, j, 0:4], y[s, j, depth - 4 :]
            at = 4 * (j % 2)
            za[s, j // 2, at : at + 4] = jnp.where(half == 0, high, low)
            zb[s, j // 2, at : at + 4] = jnp.where(half == 0, low, high)
            packed = jnp.zeros((8, width), jnp.float32)
            for g in range(depth // 8):
                turned = pltpu.roll(y[s, j, 8 * g : 8 * g + 8], 8 * g + 4, 1)
                packed = jnp.where(lane // 8 == g, turned, packed)
            xs[s, j] = packed
        return carry

    lax.fori_loop(0, count, species, 0)


VMEM = pl.BlockSpec(memory_space=pltpu.VMEM)


def pack(y):
    count, rows, depth, width = y.shape
    shapes = [(count, 4, depth, width)] * 2 + [(count, rows // 2, 8, width)] * 2
    shapes = shapes + [(count, rows, 8, width)]
    return pl.pallas_call(
        pack_body,
        out_shape=[jax.ShapeDtypeStruct(shape, jnp.float32) for shape in shapes],
        in_specs=[VMEM],
        out_specs=[VMEM] * 5,
        compiler_params=pltpu.CompilerParams(vmem_limit_bytes=14 * MIB),
        name="pack",
    )(y)


def factors(s, count):
    diff = jnp.float32(0.25 * DIFF[0])
    nu = jnp.float32(NU[0])
    for q in range(1, count):
        diff = jnp.where(s == q, jnp.float32(0.25 * DIFF[q]), diff)
        nu = jnp.where(s == q, jnp.float32(NU[q]), nu)
    return diff, nu


def rates_body(y, out):
    heat = 1.0 + 3.0 * y[2]
    out[...] = y[0] * y[1] * jnp.exp(-3.0 / heat)


def rates(y):
    return pl.pallas_call(
        rates_body,
        out_shape=jax.ShapeDtypeStruct(y.shape[1:], jnp.float32),
        in_specs=[VMEM],
        out_specs=VMEM,
        compiler_params=pltpu.CompilerParams(vmem_limit_bytes=14 * MIB),
        name="rates",
    )(y)


def along_z_body(y, vel, rate, za, zb, out, pad):
    count, rows, depth, width = y.shape
    half = lax.axis_index("zhi")

    def species(s, carry):
        diff, nu = factors(s, count)
        for j in range(rows):
            at = 4 * (j % 2)
            fa, fb = za[s, j // 2, at : at + 4], zb[s, j // 2, at : at + 4]
            pad[j, 4:8] = jnp.where(half == 0, fb, fa)
            pad[j, 8 : 8 + depth] = y[s, j]
            pad[j, 8 + depth : 12 + depth] = jnp.where(half == 0, fa, fb)
        for j in range(rows):
            centre = y[s, j]
            first = None
            second = (2.0 * C2[0]) * centre
            for k in range(1, 5):
                ahead, behind = pad[j, 8 + k : 8 + k + depth], pad[j, 8 - k : 8 - k + depth]
                term = (0.25 * C1[k - 1]) * (ahead - behind)
                first = term if first is None else first + term
                second = second + C2[k] * (ahead + behind)
            out[s, j] = centre + (diff * second - vel[2, j] * first + nu * rate[j])
        return carry

    lax.fori_loop(0, count, species, 0)


def along_z(y, *rest):
    _, rows, depth, width = y.shape
    return pl.pallas_call(
        along_z_body,
        out_shape=jax.ShapeDtypeStruct(y.shape, jnp.float32),
        in_specs=[VMEM] * (1 + len(rest)),
        out_specs=VMEM,
        scratch_shapes=[
            pltpu.VMEM((rows, depth + 16, width), jnp.float32),
        ],
        compiler_params=pltpu.CompilerParams(vmem_limit_bytes=14 * MIB),
        cost_estimate=pl.CostEstimate(
            flops=10**9, bytes_accessed=10**7, transcendentals=0
        ),
        name="along_z",
    )(y, *rest)


def along_xy_body(y, vel, base, outer, inner, xlow, xhigh, result, side, dx, pad, out, sems):
    count, rows, depth, width = y.shape
    core = lax.axis_index("core")
    below = lanes() % 8 < 4
    mh, ml = split(x_matrices(width))

    def species(s, carry):
        diff, _ = factors(s, count)
        pad[pl.ds(12 * (1 - core), 4)] = inner[s]
        pad[pl.ds(12 * core, 4)] = outer[s]
        pad[4 : 4 + rows] = y[s]
        for j in range(rows):
            packed = jnp.where(below, xlow[s, j], xhigh[s, j])
            for g in range(depth // 8):
                row = j * depth + 8 * g
                side[row : row + 8] = pltpu.roll(packed, (128 - 8 * g) % 128, 1)
        left = jnp.concatenate([y[s].reshape(rows * depth, width), side[...]], axis=1)
        high, low = split(left)
        dx[...] = dot(high, mh) + (dot(low, mh) + dot(high, ml))
        for j in range(rows):
            first = None
            second = dx[j * depth : (j + 1) * depth, width:]
            for k in range(1, 5):
                ahead, behind = pad[4 + j + k], pad[4 + j - k]
                term = (0.25 * C1[k - 1]) * (ahead - behind)
                first = term if first is None else first + term
                second = second + C2[k] * (ahead + behind)
            moved = (0.25 * vel[0, j]) * dx[j * depth : (j + 1) * depth, :width]
            out[s, j] = base[s, j] + (diff * second - (moved + vel[1, j] * first))
        pltpu.make_async_copy(out.at[s], result.at[s], sems.at[s]).start()
        return carry

    lax.fori_loop(0, count, species, 0)
    for s in range(count):
        pltpu.make_async_copy(out.at[s], result.at[s], sems.at[s]).wait()


def along_xy(y, *rest):
    _, rows, depth, width = y.shape
    return pl.pallas_call(
        along_xy_body,
        out_shape=jax.ShapeDtypeStruct(y.shape, jnp.float32),
        in_specs=[VMEM] * (1 + len(rest)),
        out_specs=pl.BlockSpec(memory_space=pl.ANY),
        scratch_shapes=[
            pltpu.VMEM((rows * depth, width), jnp.float32),
            pltpu.VMEM((rows * depth, 2 * width), jnp.float32),
            pltpu.VMEM((rows + 8, depth, width), jnp.float32),
            pltpu.VMEM(y.shape, jnp.float32),
            pltpu.SemaphoreType.DMA((y.shape[0],)),
        ],
        compiler_params=pltpu.CompilerParams(vmem_limit_bytes=16 * MIB),
        name="along_xy",
    )(y, *rest)


def products(lines):
    whole = jnp.concatenate([lines[a] for a in range(lines.shape[0])], axis=1)
    high, low = split(whole)
    turned_high, turned_low = split(whole.T)
    total = dot(turned_high, high) + (dot(turned_high, low) + dot(turned_low, high))
    return [total[a * 128 : (a + 1) * 128, b * 128 : (b + 1) * 128] for a, b in PAIRS]


def gram_body(lines, mine, other):
    core = lax.axis_index("core")
    tiles = products(lines)
    for q in range(5):
        at = slice(q * 128, (q + 1) * 128)
        mine[at] = jnp.where(core == 0, tiles[q], tiles[q + 5])
        other[at] = jnp.where(core == 0, tiles[q + 5], tiles[q])


def gram_blocks(lines):
    return pl.pallas_call(
        gram_body,
        out_shape=[jax.ShapeDtypeStruct((len(PAIRS) * 64, 128), jnp.float32)] * 2,
        in_specs=[VMEM],
        out_specs=[VMEM] * 2,
        compiler_params=pltpu.CompilerParams(vmem_limit_bytes=16 * MIB),
        name="gram",
    )(lines)


def rows_body(scale, mine, other, out, tiles, sems):
    row, core = lax.axis_index("gx"), lax.axis_index("core")

    def tile(b):
        low, top = jnp.minimum(row, b), jnp.maximum(row, b)
        index = low * 4 - (low * (low - 1)) // 2 + (top - low)
        owner = jnp.where(index >= 5, 1, 0)
        at = pl.ds(pl.multiple_of((index - 5 * owner) * 128, 128), 128)
        return owner == core, at

    for b in range(4):
        here, at = tile(b)

        @pl.when(here)
        def _():
            pltpu.make_async_copy(mine.at[at], tiles.at[b], sems.at[b]).start()

        @pl.when(jnp.logical_not(here))
        def _():
            pltpu.make_async_copy(other.at[at], tiles.at[b], sems.at[b]).start()

    for b in range(4):
        pltpu.make_async_copy(mine.at[pl.ds(0, 128)], tiles.at[b], sems.at[b]).wait()
        block = tiles[b] * scale
        out[:, b * 128 : (b + 1) * 128] = jnp.where(row <= b, block, block.T)


def gram_rows(mine, other, scale):
    return pl.pallas_call(
        functools.partial(rows_body, scale),
        out_shape=jax.ShapeDtypeStruct((128, 512), jnp.float32),
        in_specs=[pl.BlockSpec(memory_space=pl.ANY)] * 2,
        out_specs=VMEM,
        scratch_shapes=[
            pltpu.VMEM((4, 128, 128), jnp.float32),
            pltpu.SemaphoreType.DMA((4,)),
        ],
        compiler_params=pltpu.CompilerParams(vmem_limit_bytes=8 * MIB),
        name="gram_rows",
    )(mine, other)


def exchange(pieces, axes):
    return lax.all_to_all(pieces, axes, split_axis=0, concat_axis=0, tiled=True)


def gather_sum(part, axes, count):
    return jnp.sum(exchange(jnp.broadcast_to(part, (count,) + part.shape), axes), axis=0)


def shards(y, vel):
    species, rows, depth, width = y.shape
    gy, gz, gx = ("zpair", "znear", "core"), ("x", "zhi"), ("gx",)
    inner, outer, za, zb, xs = pack(y)

    def cross(count):
        return [(i, (i + 1) % count if i % 2 else (i - 1) % count) for i in range(count)]

    up = [(i, (i + 1) % 4) for i in range(4)]
    swap = [(0, 1), (1, 0)]
    za = lax.ppermute(za, "zhi", swap)
    zb = lax.ppermute(zb, gz, cross(8))
    inner = lax.ppermute(inner, "core", swap)
    outer = lax.ppermute(outer, gy, cross(16))
    xlow = lax.ppermute(xs, gx, up)
    xhigh = lax.ppermute(xs, gx, [(target, source) for source, target in up])
    base = along_z(y, vel, rates(y), za, zb)
    updated = along_xy(y, vel, base, outer, inner, xlow, xhigh)
    mine, other = gram_blocks(exchange(updated.reshape(4, species * rows * depth // 4, width), gx))
    mine = mine + lax.ppermute(other, "core", swap)
    plane = ("gx", "x")
    part = jnp.sum(exchange(mine.reshape(16, -1, 128), plane), axis=0)
    part = gather_sum(part, ("znear",), 4)
    part = gather_sum(part, ("zpair", "zhi"), 4)
    mine = exchange(jnp.broadcast_to(part, (16,) + part.shape), plane).reshape(-1, 128)
    other = lax.ppermute(mine, "core", swap)
    cells = species * rows * 16 * depth * 8
    return updated, gram_rows(mine, other, 1.0 / cells)


def solution(mesh):
    axes = ("gx", "zpair", "znear", "core", "x", "zhi")
    fine = Mesh(mesh.devices.reshape(4, 2, 4, 2, 4, 2), axes)
    grid = P(None, ("zpair", "znear", "core"), ("x", "zhi"), "gx")
    return jax.shard_map(
        shards, mesh=fine, in_specs=(grid, grid), out_specs=(grid, P("gx", None)), check_vma=False
    )
```
